256 devices in a mesh: img: 64 (over y, z, core), grp: 4 (over x).
Axes of the slice: x: 4, y: 4, z: 8, core: 2. Of those that a mesh axis runs over, the one named last changes fastest.
Arguments:
- tokens: bfloat16 [256, 96, 1024], P('img'), may hold values from -6 to 6
- embed_weight: bfloat16 [1024, 768], replicated, may hold values from -0.1875 to 0.1875
- gain_query: float32 [768], replicated, may hold values from 0.5 to 9
- gain_memory: float32 [768], replicated, may hold values from 0.5 to 9
- query_weight: bfloat16 [768, 768], replicated, may hold values from -0.5 to 0.5
- key_weight: bfloat16 [768, 768], replicated, may hold values from -0.5 to 0.5
- value_weight: bfloat16 [768, 768], replicated, may hold values from -0.21875 to 0.21875
- out_weight: bfloat16 [768, 768], replicated, may hold values from -0.21875 to 0.21875
- pair_list: int32 [9216, 2], P(('img', 'grp')), may hold values from 0 to 255, as said below
- counts: int32 [256], P(('img', 'grp')), may hold values from 27 to 36, as said below
Outputs:
- decoded: bfloat16 [9216, 96, 768], P(('img', 'grp'))
The draws below stay inside these ranges and needn't reach their ends.
Inputs may be any that keep to these rules, and one draw needn't show every extreme that they name: `pair_list`: slots p of device d are rows d * 36 to (d + 1) * 36 - 1. The query image of such a slot lies in [(d div 4) * 4, (d div 4 + 1) * 4). The memory images of one device's slots belong to owners (image div 4) that differ from one another and from d div 4. `counts`: some device has all 36 slots live.
All inputs are finite; a program needn't handle non-finite values.
Results may differ from the reference program's by a relative error of at most 0.04.
The reference program's roundings to bfloat16 on the way count: a program that leaves them out, or rounds other values in their place, can miss the bound.
Values may be sent and summed in bfloat16 or wider, within the bound.
A program may use at most 192 MiB of HBM per device.

```python
import jax
import jax.numpy as jnp
from jax import lax

D_ENC = 1024
HEADS = 12
HEAD = 64
D_DEC = 768
TOK = 96
IMG_DEV = 4
SLOTS = 36
IMAGES = 256
PAIRS = 9216
N_IMG = 64
N_GRP = 4


def shared_matrix(key):
    return jax.random.normal(key, (D_DEC, D_DEC), jnp.float32) * D_DEC ** (-0.5)


def draw_query_weight(key, part):
    common = shared_matrix(key)
    key = jax.random.fold_in(key, 3)
    private = jax.random.normal(key, (D_DEC, D_DEC), jnp.float32) * D_DEC ** (-0.5)
    return jnp.clip(0.7 * common + 0.7 * private, -0.5, 0.5).astype(jnp.bfloat16)


def draw_key_weight(key, part):
    common = shared_matrix(key)
    key = jax.random.fold_in(key, 4)
    private = jax.random.normal(key, (D_DEC, D_DEC), jnp.float32) * D_DEC ** (-0.5)
    return jnp.clip(0.7 * common + 0.7 * private, -0.5, 0.5).astype(jnp.bfloat16)


def draw_gain_query(key, part):
    key = jax.random.fold_in(key, 5)
    return jax.random.uniform(key, (D_DEC,), jnp.float32, 0.6, 1.6)


def draw_gain_memory(key, part):
    key = jax.random.fold_in(key, 6)
    return jax.random.uniform(key, (D_DEC,), jnp.float32, 0.6, 1.6)


def draw_tokens(key, part):
    key = jax.random.fold_in(key, 7)
    return jnp.clip(jax.random.normal(key, (IMAGES, TOK, D_ENC), jnp.float32), -6.0, 6.0).astype(jnp.bfloat16)


def draw_pair_list(key, part):
    key = jax.random.fold_in(key, 9)
    owner_key, local_key, query_key, place_key = jax.random.split(key, 4)
    devices_all = N_IMG * N_GRP
    column_index = jnp.arange(devices_all, dtype=jnp.int32) // N_GRP
    owner_ids = jnp.arange(N_IMG, dtype=jnp.int32)
    raw_scores = jax.random.randint(owner_key, (devices_all, N_IMG), 0, 1 << 20) * N_IMG + owner_ids[None, :] + N_IMG
    raw_scores = jnp.where(owner_ids[None, :] == 0, 0, raw_scores)
    raw_scores = jnp.where(owner_ids[None, :] == column_index[:, None], 1 << 30, raw_scores)
    picked = jnp.argsort(raw_scores, axis=1)[:, :SLOTS].astype(jnp.int32)
    least = SLOTS * 3 // 4
    position = jnp.arange(SLOTS, dtype=jnp.int32)
    target = jax.random.randint(place_key, (devices_all, 1), 0, least)
    first_owner = picked[:, 0:1]
    at_target = jnp.take_along_axis(picked, target, axis=1)
    swapped = jnp.where(position[None, :] == target, first_owner, jnp.where(position[None, :] == 0, at_target, picked))
    memory_image = swapped * IMG_DEV + jax.random.randint(local_key, (devices_all, SLOTS), 0, IMG_DEV)
    query_image = column_index[:, None] * IMG_DEV + jax.random.randint(query_key, (devices_all, SLOTS), 0, IMG_DEV)
    return jnp.stack((query_image, memory_image), axis=-1).reshape(devices_all * SLOTS, 2).astype(jnp.int32)


def draw_counts(key, part):
    key = jax.random.fold_in(key, 13)
    devices_all = N_IMG * N_GRP
    drawn = jax.random.randint(key, (devices_all,), SLOTS * 3 // 4, SLOTS + 1)
    return jnp.where(jnp.arange(devices_all) == 0, SLOTS, drawn).astype(jnp.int32)


def bell_draw(own_key, dims, spread, limit, held_as=jnp.bfloat16):
    values = spread * jax.random.normal(own_key, dims, jnp.float32)
    return jnp.clip(values, min=-limit, max=limit).astype(held_as)


def setup_inputs(seed: int = 0) -> dict:
    key_list = jax.random.split(jax.random.key(seed), 11)
    tokens = draw_tokens(jax.random.fold_in(key_list[10], 71), 0)
    embed_weight = bell_draw(key_list[1], (D_ENC, D_DEC), D_ENC ** -0.5, 0.1875)
    gain_query = draw_gain_query(jax.random.fold_in(key_list[10], 71), 0)
    gain_memory = draw_gain_memory(jax.random.fold_in(key_list[10], 71), 0)
    query_weight = draw_query_weight(jax.random.fold_in(key_list[10], 71), 0)
    key_weight = draw_key_weight(jax.random.fold_in(key_list[10], 71), 0)
    value_weight = bell_draw(key_list[6], (D_DEC, D_DEC), D_DEC ** -0.5, 0.21875)
    out_weight = bell_draw(key_list[7], (D_DEC, D_DEC), D_DEC ** -0.5, 0.21875)
    pair_list = draw_pair_list(jax.random.fold_in(key_list[10], 71), 0)
    counts = draw_counts(jax.random.fold_in(key_list[10], 71), 0)
    return dict(tokens=tokens, embed_weight=embed_weight, gain_query=gain_query, gain_memory=gain_memory, query_weight=query_weight, key_weight=key_weight, value_weight=value_weight, out_weight=out_weight, pair_list=pair_list, counts=counts)


epsilon = 1e-06

def normalize(values_in, gain_vector):
    values_in = values_in.astype(jnp.float32)
    row_mean = lax.optimization_barrier(jnp.mean(values_in, axis=-1, keepdims=True))
    centred = values_in - row_mean
    variance = lax.optimization_barrier(jnp.mean(centred * centred, axis=-1, keepdims=True))
    return centred * lax.rsqrt(variance + epsilon) * gain_vector.astype(jnp.float32)

def attend(query_rows, key_rows, value_rows, base_rows, out_weight, slot_live):
    slot_count = query_rows.shape[0]
    length = query_rows.shape[1]
    split_shape = (slot_count, length, HEADS, HEAD)
    scores = jnp.einsum('sqhd,skhd->shqk', query_rows.reshape(split_shape).astype(jnp.float32), key_rows.reshape(split_shape).astype(jnp.float32)) * HEAD ** (-0.5)
    weights = jax.nn.softmax(scores, axis=-1).astype(jnp.bfloat16)
    context = jnp.einsum('shqk,skhd->sqhd', weights.astype(jnp.float32), value_rows.reshape(split_shape).astype(jnp.float32)).astype(jnp.bfloat16)
    projected = jnp.dot(context.reshape(slot_count * length, HEADS * HEAD), out_weight, preferred_element_type=jnp.float32)
    combined = base_rows.astype(jnp.float32) + projected.reshape(slot_count, length, HEADS * HEAD)
    return jnp.where(slot_live[:, None, None], combined, jnp.float32(0.0)).astype(jnp.bfloat16)

def reference(tokens, embed_weight, gain_query, gain_memory, query_weight, key_weight, value_weight, out_weight, pair_list, counts):
    token_rows = tokens.reshape(IMAGES * TOK, D_ENC)
    embedded = jnp.dot(token_rows, embed_weight, preferred_element_type=jnp.float32).astype(jnp.bfloat16)
    query_normed = normalize(embedded, gain_query).astype(jnp.bfloat16)
    memory_normed = normalize(embedded, gain_memory).astype(jnp.bfloat16)
    queries = jnp.dot(query_normed, query_weight, preferred_element_type=jnp.float32).astype(jnp.bfloat16).reshape(IMAGES, TOK, D_DEC)
    keys_all = jnp.dot(memory_normed, key_weight, preferred_element_type=jnp.float32).astype(jnp.bfloat16).reshape(IMAGES, TOK, D_DEC)
    values_all = jnp.dot(memory_normed, value_weight, preferred_element_type=jnp.float32).astype(jnp.bfloat16).reshape(IMAGES, TOK, D_DEC)
    embedded = embedded.reshape(IMAGES, TOK, D_DEC)
    slot_index = jnp.arange(PAIRS, dtype=jnp.int32)
    slot_live = slot_index % SLOTS < counts[slot_index // SLOTS]

    def one_device(inputs):
        block_pairs, block_live = inputs
        first_image = block_pairs[:, 0]
        second_image = block_pairs[:, 1]
        return attend(jnp.take(queries, first_image, axis=0), jnp.take(keys_all, second_image, axis=0), jnp.take(values_all, second_image, axis=0), jnp.take(embedded, first_image, axis=0), out_weight, block_live)
    decoded = lax.map(one_device, (pair_list.reshape(PAIRS // SLOTS, SLOTS, 2), slot_live.reshape(PAIRS // SLOTS, SLOTS)))
    return decoded.reshape(PAIRS, TOK, D_DEC)
```

```python
import functools

import jax
import jax.numpy as jnp
from jax import lax
from jax.experimental import pallas as pl
from jax.experimental.pallas import tpu as pltpu
from jax.sharding import PartitionSpec as P

HEADS = 12
HEAD = 64
D_DEC = 768
D_ENC = 1024
TOK = 96
IMG = 4
SLOTS = 36
EPS = 1e-06

QR = TOK // 2
QC = D_DEC // 2
CH = 3
CR = QR // CH
KINDS = (2, 2, 1)
GROUP = 12

NY, NZ, NX = 4, 8, 4
MESH = pl.DeviceIdType.MESH
BF = jnp.bfloat16
F32 = jnp.float32


def build_messages():
    messages = []

    def add(name, link, size, after, **where):
        messages.append(dict(name=name, link=link, size=size, after=tuple(after), **where))

    for k in range(CH):
        quads = KINDS[k]
        hz, hy = NZ // 2, NY // 2
        az, by = [], []
        for s in range(1, hz + 1):
            for d in (1, -1):
                half = s == hz
                name = ("az", k, d, s)
                images = (0, 2) if not half else ((0, 1) if d == 1 else (1, 1))
                add(name, ("z", d), quads * images[1], [("az", k, d, s - 1)] if s > 1 else [("own", k)],
                    k=k, y=("one", 0), z=("one", -d * (s - 1)), l=images, quads=quads)
                az.append(name)
        for s in range(1, hy + 1):
            for d in (1, -1):
                half = s == hy
                name = ("by", k, d, s)
                images = (2, 2) if not half else ((2, 1) if d == 1 else (3, 1))
                add(name, ("y", d), quads * images[1], [("by", k, d, s - 1)] if s > 1 else [("own", k)],
                    k=k, y=("one", -d * (s - 1)), z=("one", 0), l=images, quads=quads)
                by.append(name)
        for s in range(1, hy + 1):
            for d in (1, -1):
                half = s == hy
                images = (0, 2) if not half else ((0, 1) if d == 1 else (1, 1))
                add(("ay", k, d, s), ("y", d), quads * images[1] * NZ, [("ay", k, d, s - 1)] if s > 1 else az,
                    k=k, y=("one", -d * (s - 1)), z=("all",), l=images, quads=quads)
        for s in range(1, hz + 1):
            for d in (1, -1):
                half = s == hz
                images = (2, 2) if not half else ((2, 1) if d == 1 else (3, 1))
                add(("bz", k, d, s), ("z", d), quads * images[1] * NY, [("bz", k, d, s - 1)] if s > 1 else by,
                    k=k, y=("all",), z=("one", -d * (s - 1)), l=images, quads=quads)
        add(("sa", k, 0), ("c", 1), quads * 2 * NZ, az, k=k, y=("one", 0), z=("all",), l=(0, 2), quads=quads)
        for s in range(1, hy):
            for d in (1, -1):
                add(("sa", k, d * s), ("c", 1), quads * 2 * NZ, [("ay", k, d, s)],
                    k=k, y=("one", -d * s), z=("all",), l=(0, 2), quads=quads)
        add(("sa", k, hy), ("c", 1), quads * 2 * NZ, [("ay", k, 1, hy), ("ay", k, -1, hy)],
            k=k, y=("one", hy), z=("all",), l=(0, 2), quads=quads)
        add(("sb", k, 0), ("c", 1), quads * 2 * NY, by, k=k, y=("all",), z=("one", 0), l=(2, 2), quads=quads)
        for s in range(1, hz):
            for d in (1, -1):
                add(("sb", k, d * s), ("c", 1), quads * 2 * NY, [("bz", k, d, s)],
                    k=k, y=("all",), z=("one", -d * s), l=(2, 2), quads=quads)
        add(("sb", k, hz), ("c", 1), quads * 2 * NY, [("bz", k, 1, hz), ("bz", k, -1, hz)],
            k=k, y=("all",), z=("one", hz), l=(2, 2), quads=quads)
        for g in range(SLOTS // GROUP):
            for d in (1, -1):
                if quads == 1:
                    add(("xf", k, d, g), ("x", d), GROUP // 2, [("sel", k)], k=k, g=g, d=d)
            for d in (1, -1):
                add(("xd", k, d, g), ("x", d), GROUP, [("sel", k)], k=k, g=g, d=d)
            if quads == 1:
                for d in (1, -1):
                    add(("xx", k, d, g), ("x", d), GROUP // 2, [("xf", k, d, g)], k=k, g=g, d=d)
    return messages


def build_order(messages):
    rate = {"x": 0.045, "y": 0.045, "z": 0.045, "c": 0.25}
    unit = CR * QC * 2 / 1e6
    done = set()
    waiting = list(messages)
    flying = []
    free = {}
    now = 0.0
    order = []

    def launch():
        rest = []
        for m in waiting:
            if all(a in done for a in m["after"]):
                start = max(now, free.get(m["link"], 0.0))
                end = start + m["size"] * unit / rate[m["link"][0]]
                free[m["link"]] = end
                flying.append((end + 1.5, len(order), m))
                order.append(("start", m["name"]))
            else:
                rest.append(m)
        waiting[:] = rest

    for k in range(CH):
        order.append(("own", k))
        done.add(("own", k))
    launch()
    need = {k: {m["name"] for m in messages if m["k"] == k and m["name"][0] in ("ay", "bz", "az", "by", "sa", "sb")}
            for k in range(CH)}
    while flying:
        flying.sort(key=lambda f: f[:2])
        t, _, m = flying.pop(0)
        now = max(now, t)
        order.append(("wait", m["name"]))
        done.add(m["name"])
        launch()
        for k in range(CH):
            if need[k] is not None and need[k] <= done:
                need[k] = None
                order.append(("sel", k))
                now += 1.0
                done.add(("sel", k))
                launch()
    assert not waiting
    return order, now


MESSAGES = build_messages()
ORDER, MODELLED = build_order(MESSAGES)
NUMBER = {m["name"]: n for n, m in enumerate(MESSAGES)}


def wrap(value, size):
    return lax.rem(value + 2 * size, size)


def exchange_kernel(tokens_ref, embed_weight_ref, want_ref, embedded_ref, memory_ref, *scratch):
    gathered, (out_going, passing, send_sem, recv_sem) = scratch[:CH], scratch[CH:]
    img = lax.axis_index("img")
    x = lax.axis_index("grp")
    y = img // (2 * NZ)
    z = lax.rem(img // 2, NZ)
    core = lax.rem(img, 2)

    def device(link):
        axis, d = link
        if axis == "x":
            return (img, wrap(x + d, NX))
        if axis == "y":
            return ((wrap(y + d, NY) * NZ + z) * 2 + core, x)
        if axis == "z":
            return ((y * NZ + wrap(z + d, NZ)) * 2 + core, x)
        return ((y * NZ + z) * 2 + (1 - core), x)

    barrier = pltpu.get_barrier_semaphore()
    partners = [("x", 1), ("x", -1), ("y", 1), ("y", -1), ("z", 1), ("z", -1), ("c", 1)]
    for link in partners:
        pl.semaphore_signal(barrier, inc=1, device_id=device(link), device_id_type=MESH)

    for n in range(IMG):
        embedded_ref[n] = jnp.dot(tokens_ref[n], embed_weight_ref[...], preferred_element_type=F32).astype(BF)

    pl.semaphore_wait(barrier, len(partners))

    def slice_of(m):
        def pick(where, at, size):
            return pl.ds(0, size) if where[0] == "all" else pl.ds(wrap(at + where[1], size), 1)

        first, count = m["l"]
        return gathered[m["k"]].at[pl.ds(0, m["quads"]), core, pick(m["y"], y, NY), pick(m["z"], z, NZ),
                           pl.ds(first, count)]

    def descriptor(name):
        n = NUMBER[name]
        m = MESSAGES[n]
        kind = name[0]
        if kind in ("xd", "xf", "xx"):
            k, g, d = m["k"], m["g"], m["d"]
            slots = pl.ds(g * GROUP, GROUP)
            half = GROUP // 2
            first = g * GROUP + (0 if d == 1 else half)
            if kind == "xd":
                src = out_going.at[k, 0 if d == 1 else 1, slots]
                dst = memory_ref.at[(-d) % NX, k, slots]
            elif kind == "xf":
                src = out_going.at[k, 2, pl.ds(first, half)]
                dst = passing.at[k, pl.ds(first, half)]
            else:
                src = passing.at[k, pl.ds(first, half)]
                dst = memory_ref.at[2, k, pl.ds(first, half)]
        else:
            src = dst = slice_of(m)
        return pltpu.make_async_remote_copy(
            src_ref=src, dst_ref=dst, send_sem=send_sem.at[n], recv_sem=recv_sem.at[n],
            device_id=device(m["link"]), device_id_type=MESH)

    def place_own(k):
        for q in range(KINDS[k]):
            quadrant = wrap(x + 2 * q, 4)
            row = pl.multiple_of((quadrant // 2) * QR + k * CR, CR)
            column = pl.multiple_of(lax.rem(quadrant, 2) * QC, 128)
            for n in range(IMG):
                gathered[k][q, core, y, z, n] = embedded_ref[n, pl.ds(row, CR), pl.ds(column, QC)]

    def select(k):
        def body(s, carry):
            def read(q, d):
                image = want_ref[wrap(x + d, NX), s]
                owner = image // IMG
                return gathered[k][q, lax.rem(owner, 2), owner // (2 * NZ), lax.rem(owner // 2, NZ),
                                   lax.rem(image, IMG)]

            out_going[k, 0, s] = read(0, 1)
            out_going[k, 1, s] = read(0, -1)
            if KINDS[k] == 1:
                out_going[k, 2, s] = read(0, 2)
            else:
                memory_ref[2, k, s] = read(1, 0)
            memory_ref[0, k, s] = read(0, 0)
            return carry

        lax.fori_loop(0, SLOTS, body, 0)

    for what, which in ORDER:
        if what == "own":
            place_own(which)
        elif what == "sel":
            select(which)
        elif what == "start":
            descriptor(which).start()
        else:
            descriptor(which).wait_recv()
    for m in MESSAGES:
        descriptor(m["name"]).wait_send()


def exchange(tokens, embed_weight, want):
    vmem = pl.BlockSpec(memory_space=pltpu.VMEM)
    return pl.pallas_call(
        exchange_kernel,
        out_shape=(
            jax.ShapeDtypeStruct((IMG, TOK, D_DEC), BF),
            jax.ShapeDtypeStruct((4, CH, SLOTS, CR, QC), BF),
        ),
        in_specs=[vmem, vmem, pl.BlockSpec(memory_space=pltpu.SMEM)],
        out_specs=(vmem, vmem),
        scratch_shapes=[
            *(pltpu.VMEM((quads, 2, NY, NZ, IMG, CR, QC), BF) for quads in KINDS),
            pltpu.VMEM((CH, 3, SLOTS, CR, QC), BF),
            pltpu.VMEM((CH, SLOTS, CR, QC), BF),
            pltpu.SemaphoreType.DMA((len(MESSAGES),)),
            pltpu.SemaphoreType.DMA((len(MESSAGES),)),
        ],
        compiler_params=pltpu.CompilerParams(
            collective_id=0, has_side_effects=True, vmem_limit_bytes=56 * 1024 * 1024
        ),
        name="exchange",
    )(tokens, embed_weight, want)


def normed(rows, gain):
    rows = rows.astype(F32)
    centred = rows - jnp.mean(rows, axis=-1, keepdims=True)
    variance = jnp.mean(centred * centred, axis=-1, keepdims=True)
    return (centred * lax.rsqrt(variance + EPS) * gain).astype(BF)


PAIRS_OF_HEADS = HEADS // 2
BATCH = 3


def decode_kernel(query_ref, count_ref, memory_ref, embedded_ref, query_weight_ref, key_weight_ref, value_weight_ref,
                  out_weight_ref, gain_query_ref, gain_memory_ref, decoded_ref, stacked, rows, context):
    step = pl.program_id(0)
    x = lax.axis_index("grp")
    lane = lax.broadcasted_iota(jnp.int32, (TOK, 2 * HEAD), 1)

    @pl.when(step == 0)
    def _():
        for n in range(IMG):
            query_rows = jnp.dot(normed(embedded_ref[n], gain_query_ref[...]), query_weight_ref[...],
                                 preferred_element_type=F32).astype(BF).astype(F32) * HEAD ** (-0.5)
            for p in range(PAIRS_OF_HEADS):
                both = query_rows[:, p * 2 * HEAD:(p + 1) * 2 * HEAD]
                stacked[n, p, :TOK] = jnp.where(lane < HEAD, both, 0.0).astype(BF)
                stacked[n, p, TOK:] = jnp.where(lane >= HEAD, both, 0.0).astype(BF)

    for b in range(BATCH):
        for quadrant in range(4):
            relative = wrap(quadrant - x, 4)
            for k in range(CH):
                row = b * TOK + (quadrant // 2) * QR + k * CR
                column = (quadrant % 2) * QC
                rows[row:row + CR, column:column + QC] = memory_ref[relative, k, b]
    memory_normed = normed(rows[...], gain_memory_ref[...])
    keys = jnp.dot(memory_normed, key_weight_ref[...], preferred_element_type=F32).astype(BF)
    values = jnp.dot(memory_normed, value_weight_ref[...], preferred_element_type=F32).astype(BF)
    for b in range(BATCH):
        image = query_ref[step * BATCH + b]
        for p in range(PAIRS_OF_HEADS):
            columns = slice(p * 2 * HEAD, (p + 1) * 2 * HEAD)
            key_pair = keys[b * TOK:(b + 1) * TOK, columns]
            value_pair = values[b * TOK:(b + 1) * TOK, columns]
            scores = lax.dot_general(stacked[image, p], key_pair, (((1,), (1,)), ((), ())),
                                     preferred_element_type=F32)
            weights = jnp.exp(scores - jnp.max(scores, axis=-1, keepdims=True))
            weights = (weights / jnp.sum(weights, axis=-1, keepdims=True)).astype(BF)
            mixed = jnp.dot(weights, value_pair, preferred_element_type=F32)
            context[b * TOK:(b + 1) * TOK, columns] = jnp.where(
                lane < HEAD, mixed[:TOK], mixed[TOK:]).astype(BF)
    projected = jnp.dot(context[...], out_weight_ref[...], preferred_element_type=F32)
    for b in range(BATCH):
        slot = step * BATCH + b
        combined = embedded_ref[query_ref[slot]].astype(F32) + projected[b * TOK:(b + 1) * TOK]
        decoded_ref[b] = jnp.where(slot < count_ref[0], combined, 0.0).astype(BF)


def decode(query_local, counts, memory, embedded, query_weight, key_weight, value_weight, out_weight, gain_query,
           gain_memory):
    def whole(*shape):
        return pl.BlockSpec(shape, lambda i, *_: (0,) * len(shape))

    return pl.pallas_call(
        decode_kernel,
        out_shape=jax.ShapeDtypeStruct((SLOTS, TOK, D_DEC), BF),
        grid_spec=pltpu.PrefetchScalarGridSpec(
            num_scalar_prefetch=2,
            grid=(SLOTS // BATCH,),
            in_specs=[
                pl.BlockSpec((4, CH, BATCH, CR, QC), lambda i, *_: (0, 0, i, 0, 0)),
                whole(IMG, TOK, D_DEC),
                whole(D_DEC, D_DEC),
                whole(D_DEC, D_DEC),
                whole(D_DEC, D_DEC),
                whole(D_DEC, D_DEC),
                whole(1, D_DEC),
                whole(1, D_DEC),
            ],
            out_specs=pl.BlockSpec((BATCH, TOK, D_DEC), lambda i, *_: (i, 0, 0)),
            scratch_shapes=[
                pltpu.VMEM((IMG, PAIRS_OF_HEADS, 2 * TOK, 2 * HEAD), BF),
                pltpu.VMEM((BATCH * TOK, D_DEC), BF),
                pltpu.VMEM((BATCH * TOK, D_DEC), BF),
            ],
        ),
        compiler_params=pltpu.CompilerParams(vmem_limit_bytes=48 * 1024 * 1024),
        name="decode",
    )(query_local, counts, memory, embedded, query_weight, key_weight, value_weight, out_weight,
      gain_query.reshape(1, -1), gain_memory.reshape(1, -1))


def on_device(
    tokens,
    embed_weight,
    gain_query,
    gain_memory,
    query_weight,
    key_weight,
    value_weight,
    out_weight,
    pair_list,
    counts,
):
    want = lax.all_gather(pair_list[:, 1], "grp", axis=0)
    embedded, memory = exchange(tokens, embed_weight, want)
    query_local = lax.rem(pair_list[:, 0], IMG)
    return decode(query_local, counts, memory, embedded, query_weight, key_weight, value_weight, out_weight,
                  gain_query, gain_memory)


def solution(mesh):
    placed = (
        P("img", None, None),
        P(),
        P(),
        P(),
        P(),
        P(),
        P(),
        P(),
        P(("img", "grp"), None),
        P(("img", "grp")),
    )
    return jax.shard_map(
        on_device,
        mesh=mesh,
        in_specs=placed,
        out_specs=P(("img", "grp"), None, None),
        check_vma=False,
    )
```

```python
import functools

import jax
import jax.numpy as jnp
from jax import lax
from jax.experimental import pallas as pl
from jax.experimental.pallas import tpu as pltpu
from jax.sharding import PartitionSpec as P

HEADS = 12
HEAD = 64
D_DEC = 768
D_ENC = 1024
TOK = 96
IMG = 4
SLOTS = 36
EPS = 1e-06

QR = TOK // 2
QC = D_DEC // 2
CH = 3
CR = QR // CH
KINDS = (1, 2, 2)
GROUP = 12

NY, NZ, NX = 4, 8, 4
MESH = pl.DeviceIdType.MESH
BF = jnp.bfloat16
F32 = jnp.float32


def build_messages():
    messages = []

    def add(name, link, size, after, **where):
        messages.append(dict(name=name, link=link, size=size, after=tuple(after), k=name[1], **where))

    hz, hy = NZ // 2, NY // 2

    def part(first, far, d):
        return (first, 2) if not far else (first + (d == -1), 1)

    for k in range(CH):
        quads = KINDS[k]
        own = ("own", k)
        along_z, along_y = {0: [own]}, {0: [own]}
        for s in range(1, hz + 1):
            for d in (1, -1):
                name, images = ("az", k, d, s), part(0, s == hz, d)
                add(name, ("z", d), quads * images[1], [("az", k, d, s - 1)] if s > 1 else [own],
                    y=("one", 0), z=("one", -d * (s - 1)), l=images)
                along_z.setdefault(hz if s == hz else -d * s, []).append(name)
        for s in range(1, hy + 1):
            for d in (1, -1):
                name, images = ("by", k, d, s), part(2, s == hy, d)
                add(name, ("y", d), quads * images[1], [("by", k, d, s - 1)] if s > 1 else [own],
                    y=("one", -d * (s - 1)), z=("one", 0), l=images)
                along_y.setdefault(hy if s == hy else -d * s, []).append(name)
        columns, planes = {}, {}
        for s in range(1, hy + 1):
            for d in (1, -1):
                images = part(0, s == hy, d)
                for at, arrived in along_z.items():
                    name = ("ay", k, d, s, at)
                    add(name, ("y", d), quads * images[1], [("ay", k, d, s - 1, at)] if s > 1 else arrived,
                        y=("one", -d * (s - 1)), z=("one", at), l=images)
                    columns.setdefault(hy if s == hy else -d * s, []).append(name)
        for s in range(1, hz + 1):
            for d in (1, -1):
                images = part(2, s == hz, d)
                for at, arrived in along_y.items():
                    name = ("bz", k, d, s, at)
                    add(name, ("z", d), quads * images[1], [("bz", k, d, s - 1, at)] if s > 1 else arrived,
                        y=("one", at), z=("one", -d * (s - 1)), l=images)
                    planes.setdefault(hz if s == hz else -d * s, []).append(name)
        columns[0] = [n for at in along_z.values() for n in at]
        planes[0] = [n for at in along_y.values() for n in at]
        for at, arrived in columns.items():
            add(("sa", k, at), ("c", 1), quads * 2 * NZ, arrived, y=("one", at), z=("all",), l=(0, 2))
        for at, arrived in planes.items():
            add(("sb", k, at), ("c", 1), quads * 2 * NY, arrived, y=("all",), z=("one", at), l=(2, 2))
        for g in range(SLOTS // GROUP):
            for d in (1, -1):
                if quads == 1:
                    add(("xf", k, d, g), ("x", d), GROUP // 2, [("sel", k)], g=g, d=d)
            for d in (1, -1):
                add(("xd", k, d, g), ("x", d), GROUP, [("sel", k)], g=g, d=d)
            if quads == 1:
                for d in (1, -1):
                    add(("xx", k, d, g), ("x", d), GROUP // 2, [("xf", k, d, g)], g=g, d=d)
    return messages


LOOK = 1.5


def build_order(messages):
    rate = {"x": 0.045, "y": 0.045, "z": 0.045, "c": 0.25}
    unit = CR * QC * 2 / 1e6
    rank = {"by": 0, "az": 0, "bz": 1, "ay": 1}
    waiting = sorted(messages, key=lambda m: (m["k"], rank.get(m["name"][0], 2)))
    done = {("own", k) for k in range(CH)}
    order = [("own", k) for k in range(CH)]
    flying, free, now = [], {}, 0.0

    def launch():
        rest = []
        for m in waiting:
            at = free.get(m["link"], 0.0)
            if at - now < LOOK and all(a in done for a in m["after"]):
                end = max(now, at) + m["size"] * unit / rate[m["link"][0]]
                free[m["link"]] = end
                flying.append((end + 1.5, len(order), m))
                order.append(("start", m["name"]))
            else:
                rest.append(m)
        waiting[:] = rest

    launch()
    need = {k: {m["name"] for m in messages if m["k"] == k and m["link"][0] != "x"} for k in range(CH)}
    while flying or waiting:
        if not flying:
            now += 0.5
            launch()
            continue
        flying.sort(key=lambda f: f[:2])
        t, _, m = flying.pop(0)
        now = max(now, t) + 0.05
        order.append(("wait", m["name"]))
        done.add(m["name"])
        launch()
        for k in range(CH):
            if need[k] is not None and need[k] <= done:
                need[k] = None
                order.append(("sel", k))
                now += 1.0
                done.add(("sel", k))
                launch()
    return order, now


MESSAGES = build_messages()
ORDER, MODELLED = build_order(MESSAGES)
NUMBER = {m["name"]: n for n, m in enumerate(MESSAGES)}


def wrap(value, size):
    return lax.rem(value + 2 * size, size)


def exchange_kernel(tokens_ref, embed_weight_ref, want_ref, embedded_ref, memory_ref, *scratch):
    gathered, (out_going, passing, send_sem, recv_sem) = scratch[:CH], scratch[CH:]
    img = lax.axis_index("img")
    x = lax.axis_index("grp")
    y = img // (2 * NZ)
    z = lax.rem(img // 2, NZ)
    core = lax.rem(img, 2)

    def device(link):
        axis, d = link
        if axis == "x":
            return (img, wrap(x + d, NX))
        if axis == "y":
            return ((wrap(y + d, NY) * NZ + z) * 2 + core, x)
        if axis == "z":
            return ((y * NZ + wrap(z + d, NZ)) * 2 + core, x)
        return ((y * NZ + z) * 2 + (1 - core), x)

    barrier = pltpu.get_barrier_semaphore()
    partners = [("x", 1), ("x", -1), ("y", 1), ("y", -1), ("z", 1), ("z", -1), ("c", 1)]
    for link in partners:
        pl.semaphore_signal(barrier, inc=1, device_id=device(link), device_id_type=MESH)

    for n in range(IMG):
        embedded_ref[n] = jnp.dot(tokens_ref[n], embed_weight_ref[...], preferred_element_type=F32).astype(BF)

    pl.semaphore_wait(barrier, len(partners))

    def slice_of(m):
        def pick(where, at, size):
            return pl.ds(0, size) if where[0] == "all" else pl.ds(wrap(at + where[1], size), 1)

        first, count = m["l"]
        return gathered[m["k"]].at[pl.ds(0, KINDS[m["k"]]), core, pick(m["y"], y, NY), pick(m["z"], z, NZ),
                           pl.ds(first, count)]

    def descriptor(name):
        n = NUMBER[name]
        m = MESSAGES[n]
        kind = name[0]
        if kind in ("xd", "xf", "xx"):
            k, g, d = m["k"], m["g"], m["d"]
            slots = pl.ds(g * GROUP, GROUP)
            half = GROUP // 2
            first = g * GROUP + (0 if d == 1 else half)
            if kind == "xd":
                src = out_going.at[k, 0 if d == 1 else 1, slots]
                dst = memory_ref.at[(-d) % NX, k, slots]
            elif kind == "xf":
                src = out_going.at[k, 2, pl.ds(first, half)]
                dst = passing.at[k, pl.ds(first, half)]
            else:
                src = passing.at[k, pl.ds(first, half)]
                dst = memory_ref.at[2, k, pl.ds(first, half)]
        else:
            src = dst = slice_of(m)
        return pltpu.make_async_remote_copy(
            src_ref=src, dst_ref=dst, send_sem=send_sem.at[n], recv_sem=recv_sem.at[n],
            device_id=device(m["link"]), device_id_type=MESH)

    def place_own(k):
        for q in range(KINDS[k]):
            quadrant = wrap(x + 2 * q, 4)
            row = pl.multiple_of((quadrant // 2) * QR + k * CR, CR)
            column = pl.multiple_of(lax.rem(quadrant, 2) * QC, 128)
            for n in range(IMG):
                gathered[k][q, core, y, z, n] = embedded_ref[n, pl.ds(row, CR), pl.ds(column, QC)]

    def select(k):
        def body(s, carry):
            def read(q, d):
                image = want_ref[wrap(x + d, NX), s]
                owner = image // IMG
                return gathered[k][q, lax.rem(owner, 2), owner // (2 * NZ), lax.rem(owner // 2, NZ),
                                   lax.rem(image, IMG)]

            out_going[k, 0, s] = read(0, 1)
            out_going[k, 1, s] = read(0, -1)
            if KINDS[k] == 1:
                out_going[k, 2, s] = read(0, 2)
            else:
                memory_ref[2, k, s] = read(1, 0)
            memory_ref[0, k, s] = read(0, 0)
            return carry

        lax.fori_loop(0, SLOTS, body, 0)

    for what, which in ORDER:
        if what == "own":
            place_own(which)
        elif what == "sel":
            select(which)
        elif what == "start":
            descriptor(which).start()
        else:
            descriptor(which).wait_recv()
    for m in MESSAGES:
        descriptor(m["name"]).wait_send()


def exchange(tokens, embed_weight, want):
    vmem = pl.BlockSpec(memory_space=pltpu.VMEM)
    return pl.pallas_call(
        exchange_kernel,
        out_shape=(
            jax.ShapeDtypeStruct((IMG, TOK, D_DEC), BF),
            jax.ShapeDtypeStruct((4, CH, SLOTS, CR, QC), BF),
        ),
        in_specs=[vmem, vmem, pl.BlockSpec(memory_space=pltpu.SMEM)],
        out_specs=(vmem, vmem),
        scratch_shapes=[
            *(pltpu.VMEM((quads, 2, NY, NZ, IMG, CR, QC), BF) for quads in KINDS),
            pltpu.VMEM((CH, 3, SLOTS, CR, QC), BF),
            pltpu.VMEM((CH, SLOTS, CR, QC), BF),
            pltpu.SemaphoreType.DMA((len(MESSAGES),)),
            pltpu.SemaphoreType.DMA((len(MESSAGES),)),
        ],
        compiler_params=pltpu.CompilerParams(
            collective_id=0, has_side_effects=True, vmem_limit_bytes=56 * 1024 * 1024
        ),
        name="exchange",
    )(tokens, embed_weight, want)


def normed(rows, gain):
    rows = rows.astype(F32)
    centred = rows - jnp.mean(rows, axis=-1, keepdims=True)
    variance = jnp.mean(centred * centred, axis=-1, keepdims=True)
    return (centred * lax.rsqrt(variance + EPS) * gain).astype(BF)


PAIRS_OF_HEADS = HEADS // 2
BATCH = 3


def decode_kernel(query_ref, count_ref, memory_ref, embedded_ref, query_weight_ref, key_weight_ref, value_weight_ref,
                  out_weight_ref, gain_query_ref, gain_memory_ref, decoded_ref, stacked, rows, context):
    step = pl.program_id(0)
    x = lax.axis_index("grp")
    lane = lax.broadcasted_iota(jnp.int32, (TOK, 2 * HEAD), 1)

    @pl.when(step == 0)
    def _():
        for n in range(IMG):
            query_rows = jnp.dot(normed(embedded_ref[n], gain_query_ref[...]), query_weight_ref[...],
                                 preferred_element_type=F32).astype(BF).astype(F32) * HEAD ** (-0.5)
            for p in range(PAIRS_OF_HEADS):
                both = query_rows[:, p * 2 * HEAD:(p + 1) * 2 * HEAD]
                stacked[n, p, :TOK] = jnp.where(lane < HEAD, both, 0.0).astype(BF)
                stacked[n, p, TOK:] = jnp.where(lane >= HEAD, both, 0.0).astype(BF)

    for b in range(BATCH):
        for quadrant in range(4):
            relative = wrap(quadrant - x, 4)
            for k in range(CH):
                row = b * TOK + (quadrant // 2) * QR + k * CR
                column = (quadrant % 2) * QC
                rows[row:row + CR, column:column + QC] = memory_ref[relative, k, b]
    memory_normed = normed(rows[...], gain_memory_ref[...])
    keys = jnp.dot(memory_normed, key_weight_ref[...], preferred_element_type=F32).astype(BF)
    values = jnp.dot(memory_normed, value_weight_ref[...], preferred_element_type=F32).astype(BF)
    for b in range(BATCH):
        image = query_ref[step * BATCH + b]
        for p in range(PAIRS_OF_HEADS):
            columns = slice(p * 2 * HEAD, (p + 1) * 2 * HEAD)
            key_pair = keys[b * TOK:(b + 1) * TOK, columns]
            value_pair = values[b * TOK:(b + 1) * TOK, columns]
            scores = lax.dot_general(stacked[image, p], key_pair, (((1,), (1,)), ((), ())),
                                     preferred_element_type=F32)
            weights = jnp.exp(scores - jnp.max(scores, axis=-1, keepdims=True))
            weights = (weights / jnp.sum(weights, axis=-1, keepdims=True)).astype(BF)
            mixed = jnp.dot(weights, value_pair, preferred_element_type=F32)
            context[b * TOK:(b + 1) * TOK, columns] = jnp.where(
                lane < HEAD, mixed[:TOK], mixed[TOK:]).astype(BF)
    projected = jnp.dot(context[...], out_weight_ref[...], preferred_element_type=F32)
    for b in range(BATCH):
        slot = step * BATCH + b
        combined = embedded_ref[query_ref[slot]].astype(F32) + projected[b * TOK:(b + 1) * TOK]
        decoded_ref[b] = jnp.where(slot < count_ref[0], combined, 0.0).astype(BF)


def decode(query_local, counts, memory, embedded, query_weight, key_weight, value_weight, out_weight, gain_query,
           gain_memory):
    def whole(*shape):
        return pl.BlockSpec(shape, lambda i, *_: (0,) * len(shape))

    return pl.pallas_call(
        decode_kernel,
        out_shape=jax.ShapeDtypeStruct((SLOTS, TOK, D_DEC), BF),
        grid_spec=pltpu.PrefetchScalarGridSpec(
            num_scalar_prefetch=2,
            grid=(SLOTS // BATCH,),
            in_specs=[
                pl.BlockSpec((4, CH, BATCH, CR, QC), lambda i, *_: (0, 0, i, 0, 0)),
                whole(IMG, TOK, D_DEC),
                whole(D_DEC, D_DEC),
                whole(D_DEC, D_DEC),
                whole(D_DEC, D_DEC),
                whole(D_DEC, D_DEC),
                whole(1, D_DEC),
                whole(1, D_DEC),
            ],
            out_specs=pl.BlockSpec((BATCH, TOK, D_DEC), lambda i, *_: (i, 0, 0)),
            scratch_shapes=[
                pltpu.VMEM((IMG, PAIRS_OF_HEADS, 2 * TOK, 2 * HEAD), BF),
                pltpu.VMEM((BATCH * TOK, D_DEC), BF),
                pltpu.VMEM((BATCH * TOK, D_DEC), BF),
            ],
        ),
        compiler_params=pltpu.CompilerParams(vmem_limit_bytes=48 * 1024 * 1024),
        name="decode",
    )(query_local, counts, memory, embedded, query_weight, key_weight, value_weight, out_weight,
      gain_query.reshape(1, -1), gain_memory.reshape(1, -1))


def on_device(
    tokens,
    embed_weight,
    gain_query,
    gain_memory,
    query_weight,
    key_weight,
    value_weight,
    out_weight,
    pair_list,
    counts,
):
    want = lax.all_gather(pair_list[:, 1], "grp", axis=0)
    embedded, memory = exchange(tokens, embed_weight, want)
    query_local = lax.rem(pair_list[:, 0], IMG)
    return decode(query_local, counts, memory, embedded, query_weight, key_weight, value_weight, out_weight,
                  gain_query, gain_memory)


def solution(mesh):
    placed = (
        P("img", None, None),
        P(),
        P(),
        P(),
        P(),
        P(),
        P(),
        P(),
        P(("img", "grp"), None),
        P(("img", "grp")),
    )
    return jax.shard_map(
        on_device,
        mesh=mesh,
        in_specs=placed,
        out_specs=P(("img", "grp"), None, None),
        check_vma=False,
    )
```

```python
import functools

import jax
import jax.numpy as jnp
from jax import lax
from jax.experimental import pallas as pl
from jax.experimental.pallas import tpu as pltpu
from jax.sharding import PartitionSpec as P

HEADS = 12
HEAD = 64
D_DEC = 768
D_ENC = 1024
TOK = 96
IMG = 4
SLOTS = 36
EPS = 1e-06

QR = TOK // 2
QC = D_DEC // 2
CH = 3
CR = QR // CH
KINDS = (1, 2, 2)
GROUP = 12

NY, NZ, NX = 4, 8, 4
MESH = pl.DeviceIdType.MESH
BF = jnp.bfloat16
F32 = jnp.float32


def build_messages():
    messages = []
    for d in (1, -1, 2):
        messages.append(dict(name=("wt", 0, d), link=("x", d), size=0.5, after=(), k=0, d=d))

    def add(name, link, size, after, **where):
        messages.append(dict(name=name, link=link, size=size, after=tuple(after), k=name[1], **where))

    hz, hy = NZ // 2, NY // 2

    def part(first, far, d):
        return (first, 2) if not far else (first + (d == -1), 1)

    for k in range(CH):
        quads = KINDS[k]
        own = ("own", k)
        along_z, along_y = {0: [own]}, {0: [own]}
        for s in range(1, hz + 1):
            for d in (1, -1):
                name, images = ("az", k, d, s), part(0, s == hz, d)
                add(name, ("z", d), quads * images[1], [("az", k, d, s - 1)] if s > 1 else [own],
                    y=("one", 0), z=("one", -d * (s - 1)), l=images)
                along_z.setdefault(hz if s == hz else -d * s, []).append(name)
        for s in range(1, hy + 1):
            for d in (1, -1):
                name, images = ("by", k, d, s), part(2, s == hy, d)
                add(name, ("y", d), quads * images[1], [("by", k, d, s - 1)] if s > 1 else [own],
                    y=("one", -d * (s - 1)), z=("one", 0), l=images)
                along_y.setdefault(hy if s == hy else -d * s, []).append(name)
        columns, planes = {}, {}
        for s in range(1, hy + 1):
            for d in (1, -1):
                images = part(0, s == hy, d)
                for at, arrived in along_z.items():
                    name = ("ay", k, d, s, at)
                    add(name, ("y", d), quads * images[1], [("ay", k, d, s - 1, at)] if s > 1 else arrived,
                        y=("one", -d * (s - 1)), z=("one", at), l=images)
                    columns.setdefault(hy if s == hy else -d * s, []).append(name)
        for s in range(1, hz + 1):
            for d in (1, -1):
                images = part(2, s == hz, d)
                for at, arrived in along_y.items():
                    name = ("bz", k, d, s, at)
                    add(name, ("z", d), quads * images[1], [("bz", k, d, s - 1, at)] if s > 1 else arrived,
                        y=("one", at), z=("one", -d * (s - 1)), l=images)
                    planes.setdefault(hz if s == hz else -d * s, []).append(name)
        columns[0] = [n for at in along_z.values() for n in at]
        planes[0] = [n for at in along_y.values() for n in at]
        for at, arrived in columns.items():
            add(("sa", k, at), ("c", 1), quads * 2 * NZ, arrived, y=("one", at), z=("all",), l=(0, 2))
        for at, arrived in planes.items():
            add(("sb", k, at), ("c", 1), quads * 2 * NY, arrived, y=("all",), z=("one", at), l=(2, 2))
        for g in range(SLOTS // GROUP):
            for d in (1, -1):
                if quads == 1:
                    add(("xf", k, d, g), ("x", d), GROUP // 2, [("sel", k)], g=g, d=d)
            for d in (1, -1):
                add(("xd", k, d, g), ("x", d), GROUP, [("sel", k)], g=g, d=d)
            if quads == 1:
                for d in (1, -1):
                    add(("xx", k, d, g), ("x", d), GROUP // 2, [("xf", k, d, g)], g=g, d=d)
    return messages


LOOK = 2.0
COST = {"sel": 1.0, "queries": 2.0, "kv": 1.6, "attend": 7.0, "want": 1.0}


def build_order(messages):
    rate = {"x": 0.045, "y": 0.045, "z": 0.045, "c": 0.25}
    unit = CR * QC * 2 / 1e6
    rank = {"wt": -1, "by": 0, "az": 0, "bz": 1, "ay": 1}
    waiting = sorted(messages, key=lambda m: (m["k"], rank.get(m["name"][0], 2)))
    done = {("own", k) for k in range(CH)}
    order = [("own", k) for k in range(CH)]
    flying, free, now = [], {}, 0.0
    groups = range(SLOTS // GROUP)
    steps = [(("want",), {("wt", 0, d) for d in (1, -1, 2)})]
    for k in range(CH):
        gather = {m["name"] for m in messages if m["k"] == k and m["link"][0] != "x"}
        steps.append((("sel", k), gather | {("want",)}))
    steps.append((("queries",), set()))
    for k in range(CH):
        for g in groups:
            here = {m["name"] for m in messages if m["k"] == k and m.get("g") == g and m["name"][0] in ("xd", "xx")}
            steps.append((("kv", k, g), here | {("sel", k)}))
    for g in groups:
        steps.append((("attend", g), {("kv", k, g) for k in range(CH)} | {("queries",)}))

    def launch():
        rest = []
        for m in waiting:
            at = free.get(m["link"], 0.0)
            if at - now < LOOK and all(a in done for a in m["after"]):
                end = max(now, at) + m["size"] * unit / rate[m["link"][0]]
                free[m["link"]] = end
                flying.append((end + 1.5, len(order), m))
                order.append(("start", m["name"]))
            else:
                rest.append(m)
        waiting[:] = rest

    launch()
    while flying or waiting or steps:
        flying.sort(key=lambda f: f[:2])
        ready = [step for step in steps if step[1] <= done]
        if ready and (ready[0][0][0] in ("sel", "want") or not flying or flying[0][0] > now + 0.3):
            name = ready[0][0]
            steps.remove(ready[0])
            order.append(name)
            now += COST[name[0]]
            done.add(name)
        elif flying:
            t, _, m = flying.pop(0)
            now = max(now, t) + 0.05
            order.append(("wait", m["name"]))
            done.add(m["name"])
        else:
            now += 0.5
        launch()
    return order, now


MESSAGES = build_messages()
ORDER, MODELLED = build_order(MESSAGES)
NUMBER = {m["name"]: n for n, m in enumerate(MESSAGES)}


def wrap(value, size):
    return lax.rem(value + 2 * size, size)


def normed(rows, gain):
    rows = rows.astype(F32)
    centred = rows - jnp.mean(rows, axis=-1, keepdims=True)
    variance = jnp.mean(centred * centred, axis=-1, keepdims=True)
    return (centred * lax.rsqrt(variance + EPS) * gain).astype(BF)


PAIRS_OF_HEADS = HEADS // 2
BATCH = 3


def decode_kernel(tokens_ref, embed_weight_ref, gain_query_ref, gain_memory_ref, query_weight_hbm, key_weight_hbm,
                  value_weight_hbm, out_weight_hbm, pairs_ref, count_ref, decoded_hbm, *scratch):
    gathered = scratch[:CH]
    (out_going, passing, memory, embedded, want_vmem, want, weights_vmem, stacked, rows, keys, values, context,
     send_sem, recv_sem, local_sem) = scratch[CH:]
    img = lax.axis_index("img")
    x = lax.axis_index("grp")
    y = img // (2 * NZ)
    z = lax.rem(img // 2, NZ)
    core = lax.rem(img, 2)

    def device(link):
        axis, d = link
        if axis == "x":
            return (img, wrap(x + d, NX))
        if axis == "y":
            return ((wrap(y + d, NY) * NZ + z) * 2 + core, x)
        if axis == "z":
            return ((y * NZ + wrap(z + d, NZ)) * 2 + core, x)
        return ((y * NZ + z) * 2 + (1 - core), x)

    barrier = pltpu.get_barrier_semaphore()
    partners = [("x", 1), ("x", -1), ("x", 2), ("y", 1), ("y", -1), ("z", 1), ("z", -1), ("c", 1)]
    for link in partners:
        pl.semaphore_signal(barrier, inc=1, device_id=device(link), device_id_type=MESH)

    loads = [pltpu.make_async_copy(hbm, weights_vmem.at[n], local_sem.at[n])
             for n, hbm in enumerate((query_weight_hbm, key_weight_hbm, value_weight_hbm, out_weight_hbm))]
    for load in loads:
        load.start()

    want_vmem[0] = jnp.zeros_like(want_vmem[0])
    want_vmem[0, :SLOTS, :2] = pairs_ref[...]
    for n in range(IMG):
        embedded[n] = jnp.dot(tokens_ref[n], embed_weight_ref[...], preferred_element_type=F32).astype(BF)

    pl.semaphore_wait(barrier, len(partners))

    def slice_of(m):
        def pick(where, at, size):
            return pl.ds(0, size) if where[0] == "all" else pl.ds(wrap(at + where[1], size), 1)

        first, count = m["l"]
        return gathered[m["k"]].at[pl.ds(0, KINDS[m["k"]]), core, pick(m["y"], y, NY), pick(m["z"], z, NZ),
                                   pl.ds(first, count)]

    def descriptor(name):
        n = NUMBER[name]
        m = MESSAGES[n]
        kind = name[0]
        half = GROUP // 2
        if kind == "wt":
            src = want_vmem.at[0]
            dst = want_vmem.at[(-m["d"]) % NX]
        elif kind in ("xd", "xf", "xx"):
            k, g, d = m["k"], m["g"], m["d"]
            slots = pl.ds(g * GROUP, GROUP)
            some = pl.ds(g * GROUP + (0 if d == 1 else half), half)
            if kind == "xd":
                src = out_going.at[k, 0 if d == 1 else 1, slots]
                dst = memory.at[(-d) % NX, k, slots]
            elif kind == "xf":
                src = out_going.at[k, 2, some]
                dst = passing.at[k, some]
            else:
                src = passing.at[k, some]
                dst = memory.at[2, k, some]
        else:
            src = dst = slice_of(m)
        return pltpu.make_async_remote_copy(
            src_ref=src, dst_ref=dst, send_sem=send_sem.at[n], recv_sem=recv_sem.at[n],
            device_id=device(m["link"]), device_id_type=MESH)

    def place_own(k):
        for q in range(KINDS[k]):
            quadrant = wrap(x + 2 * q, 4)
            row = pl.multiple_of((quadrant // 2) * QR + k * CR, CR)
            column = pl.multiple_of(lax.rem(quadrant, 2) * QC, 128)
            for n in range(IMG):
                gathered[k][q, core, y, z, n] = embedded[n, pl.ds(row, CR), pl.ds(column, QC)]

    def read_wants():
        move = pltpu.make_async_copy(want_vmem, want, local_sem.at[4])
        move.start()
        move.wait()

    def select(k):
        def body(s, carry):
            def read(q, d):
                image = want[d % NX, s, 1]
                owner = image // IMG
                return gathered[k][q, lax.rem(owner, 2), owner // (2 * NZ), lax.rem(owner // 2, NZ),
                                   lax.rem(image, IMG)]

            out_going[k, 0, s] = read(0, 1)
            out_going[k, 1, s] = read(0, -1)
            if KINDS[k] == 1:
                out_going[k, 2, s] = read(0, 2)
            else:
                memory[2, k, s] = read(1, 0)
            memory[0, k, s] = read(0, 0)
            return carry

        lax.fori_loop(0, SLOTS, body, 0)

    lane = lax.broadcasted_iota(jnp.int32, (TOK, 2 * HEAD), 1)

    def make_queries():
        for load in loads:
            load.wait()

        def body(n, carry):
            query_rows = jnp.dot(normed(embedded[n], gain_query_ref[...]), weights_vmem[0],
                                 preferred_element_type=F32).astype(BF).astype(F32) * HEAD ** (-0.5)
            for p in range(PAIRS_OF_HEADS):
                both = query_rows[:, p * 2 * HEAD:(p + 1) * 2 * HEAD]
                stacked[n, p, :TOK] = jnp.where(lane < HEAD, both, 0.0).astype(BF)
                stacked[n, p, TOK:] = jnp.where(lane >= HEAD, both, 0.0).astype(BF)
            return carry

        lax.fori_loop(0, IMG, body, 0)

    def project(k, g):
        slots = pl.ds(g * GROUP, GROUP)
        for quadrant in range(4):
            part = memory[wrap(quadrant - x, 4), k, slots]
            rows[:, (quadrant // 2) * CR:(quadrant // 2 + 1) * CR, (quadrant % 2) * QC:(quadrant % 2 + 1) * QC] = part
        here = normed(rows[...].reshape(GROUP * 2 * CR, D_DEC), gain_memory_ref[...])
        for n, result in ((1, keys), (2, values)):
            made = jnp.dot(here, weights_vmem[n], preferred_element_type=F32).astype(BF)
            result[slots, 2 * CR * k:2 * CR * (k + 1)] = made.reshape(GROUP, 2 * CR, D_DEC)

    def attend(g):
        def body(i, carry):
            first = g * GROUP + i * BATCH
            for b in range(BATCH):
                slot = first + b
                image = lax.rem(want[0, slot, 0], IMG)
                for p in range(PAIRS_OF_HEADS):
                    columns = slice(p * 2 * HEAD, (p + 1) * 2 * HEAD)
                    scores = lax.dot_general(stacked[image, p], keys[slot, :, columns], (((1,), (1,)), ((), ())),
                                             preferred_element_type=F32)
                    powers = jnp.exp(scores - jnp.max(scores, axis=-1, keepdims=True))
                    share = 1.0 / jnp.sum(powers, axis=-1, keepdims=True)
                    mixed = jnp.dot((powers * share).astype(BF), values[slot, :, columns],
                                    preferred_element_type=F32)
                    context[b * TOK:(b + 1) * TOK, columns] = jnp.where(
                        lane < HEAD, mixed[:TOK], mixed[TOK:]).astype(BF)
            projected = jnp.dot(context[...], weights_vmem[3], preferred_element_type=F32)
            for b in range(BATCH):
                slot = first + b
                image = lax.rem(want[0, slot, 0], IMG)
                combined = embedded[image].astype(F32) + projected[b * TOK:(b + 1) * TOK]
                keys[slot] = jnp.where(slot < count_ref[0], combined, 0.0).astype(BF)
            return carry

        lax.fori_loop(0, GROUP // BATCH, body, 0)
        result(g).start()

    def result(g):
        slots = pl.ds(g * GROUP, GROUP)
        return pltpu.make_async_copy(keys.at[slots], decoded_hbm.at[slots], local_sem.at[5 + g])

    run = dict(own=place_own, want=read_wants, sel=select, queries=make_queries, kv=project, attend=attend,
               start=lambda name: descriptor(name).start(), wait=lambda name: descriptor(name).wait_recv())
    for what, *which in ORDER:
        run[what](*which)
    for m in MESSAGES:
        descriptor(m["name"]).wait_send()
    for g in range(SLOTS // GROUP):
        result(g).wait()


def decode(tokens, embed_weight, gain_query, gain_memory, query_weight, key_weight, value_weight, out_weight, pairs,
           counts):
    vmem = pl.BlockSpec(memory_space=pltpu.VMEM)
    hbm = pl.BlockSpec(memory_space=pl.ANY)
    return pl.pallas_call(
        decode_kernel,
        out_shape=jax.ShapeDtypeStruct((SLOTS, TOK, D_DEC), BF),
        in_specs=[vmem, vmem, vmem, vmem, hbm, hbm, hbm, hbm, vmem, pl.BlockSpec(memory_space=pltpu.SMEM)],
        out_specs=hbm,
        scratch_shapes=[
            *(pltpu.VMEM((quads, 2, NY, NZ, IMG, CR, QC), BF) for quads in KINDS),
            pltpu.VMEM((CH, 3, SLOTS, CR, QC), BF),
            pltpu.VMEM((CH, SLOTS, CR, QC), BF),
            pltpu.VMEM((4, CH, SLOTS, CR, QC), BF),
            pltpu.VMEM((IMG, TOK, D_DEC), BF),
            pltpu.VMEM((NX, 40, 128), jnp.int32),
            pltpu.SMEM((NX, 40, 128), jnp.int32),
            pltpu.VMEM((4, D_DEC, D_DEC), BF),
            pltpu.VMEM((IMG, PAIRS_OF_HEADS, 2 * TOK, 2 * HEAD), BF),
            pltpu.VMEM((GROUP, 2 * CR, D_DEC), BF),
            pltpu.VMEM((SLOTS, TOK, D_DEC), BF),
            pltpu.VMEM((SLOTS, TOK, D_DEC), BF),
            pltpu.VMEM((BATCH * TOK, D_DEC), BF),
            pltpu.SemaphoreType.DMA((len(MESSAGES),)),
            pltpu.SemaphoreType.DMA((len(MESSAGES),)),
            pltpu.SemaphoreType.DMA((5 + SLOTS // GROUP,)),
        ],
        compiler_params=pltpu.CompilerParams(
            collective_id=0, has_side_effects=True, vmem_limit_bytes=60 * 1024 * 1024
        ),
        name="decode",
    )(tokens, embed_weight, gain_query, gain_memory, query_weight, key_weight, value_weight, out_weight, pairs, counts)


def on_device(
    tokens,
    embed_weight,
    gain_query,
    gain_memory,
    query_weight,
    key_weight,
    value_weight,
    out_weight,
    pair_list,
    counts,
):
    return decode(tokens, embed_weight, gain_query, gain_memory, query_weight, key_weight, value_weight, out_weight,
                  pair_list, counts)


def solution(mesh):
    placed = (
        P("img", None, None),
        P(),
        P(),
        P(),
        P(),
        P(),
        P(),
        P(),
        P(("img", "grp"), None),
        P(("img", "grp")),
    )
    return jax.shard_map(
        on_device,
        mesh=mesh,
        in_specs=placed,
        out_specs=P(("img", "grp"), None, None),
        check_vma=False,
    )
```

```python
import functools

import jax
import jax.numpy as jnp
from jax import lax
from jax.experimental import pallas as pl
from jax.experimental.pallas import tpu as pltpu
from jax.sharding import PartitionSpec as P

HEADS = 12
HEAD = 64
D_DEC = 768
D_ENC = 1024
TOK = 96
IMG = 4
SLOTS = 36
EPS = 1e-06

QR = TOK // 2
QC = D_DEC // 2
CH = 3
CR = QR // CH
KINDS = (1, 2, 2)
GROUP = 12

NY, NZ, NX = 4, 8, 4
MESH = pl.DeviceIdType.MESH
BF = jnp.bfloat16
F32 = jnp.float32


def build_messages():
    messages = []
    for d in (1, -1, 2):
        messages.append(dict(name=("wt", 0, d), link=("x", d), size=0.5, after=(), k=0, d=d))

    def add(name, link, size, after, **where):
        messages.append(dict(name=name, link=link, size=size, after=tuple(after), k=name[1], **where))

    hz, hy = NZ // 2, NY // 2

    def part(first, far, d):
        return (first, 2) if not far else (first + (d == -1), 1)

    for k in range(CH):
        quads = KINDS[k]
        own = ("own", k)
        along_z, along_y = {0: [own]}, {0: [own]}
        for s in range(1, hz + 1):
            for d in (1, -1):
                name, images = ("az", k, d, s), part(0, s == hz, d)
                add(name, ("z", d), quads * images[1], [("az", k, d, s - 1)] if s > 1 else [own],
                    y=("one", 0), z=("one", -d * (s - 1)), l=images)
                along_z.setdefault(hz if s == hz else -d * s, []).append(name)
        for s in range(1, hy + 1):
            for d in (1, -1):
                name, images = ("by", k, d, s), part(2, s == hy, d)
                add(name, ("y", d), quads * images[1], [("by", k, d, s - 1)] if s > 1 else [own],
                    y=("one", -d * (s - 1)), z=("one", 0), l=images)
                along_y.setdefault(hy if s == hy else -d * s, []).append(name)
        columns, planes = {}, {}
        for s in range(1, hy + 1):
            for d in (1, -1):
                images = part(0, s == hy, d)
                for at, arrived in along_z.items():
                    name = ("ay", k, d, s, at)
                    add(name, ("y", d), quads * images[1], [("ay", k, d, s - 1, at)] if s > 1 else arrived,
                        y=("one", -d * (s - 1)), z=("one", at), l=images)
                    columns.setdefault(hy if s == hy else -d * s, []).append(name)
        for s in range(1, hz + 1):
            for d in (1, -1):
                images = part(2, s == hz, d)
                for at, arrived in along_y.items():
                    name = ("bz", k, d, s, at)
                    add(name, ("z", d), quads * images[1], [("bz", k, d, s - 1, at)] if s > 1 else arrived,
                        y=("one", at), z=("one", -d * (s - 1)), l=images)
                    planes.setdefault(hz if s == hz else -d * s, []).append(name)
        columns[0] = [n for at in along_z.values() for n in at]
        planes[0] = [n for at in along_y.values() for n in at]
        for at, arrived in columns.items():
            add(("sa", k, at), ("c", 1), quads * 2 * NZ, arrived, y=("one", at), z=("all",), l=(0, 2))
        for at, arrived in planes.items():
            add(("sb", k, at), ("c", 1), quads * 2 * NY, arrived, y=("all",), z=("one", at), l=(2, 2))
        for g in range(SLOTS // GROUP):
            for d in (1, -1):
                if quads == 1:
                    add(("xf", k, d, g), ("x", d), GROUP // 2, [("sel", k)], g=g, d=d)
            for d in (1, -1):
                add(("xd", k, d, g), ("x", d), GROUP, [("sel", k)], g=g, d=d)
            if quads == 1:
                for d in (1, -1):
                    add(("xx", k, d, g), ("x", d), GROUP // 2, [("xf", k, d, g)], g=g, d=d)
    return messages


LOOK = 2.0
COST = {"sel": 1.0, "queries": 2.0, "kv": 1.6, "attend": 7.0, "want": 1.0}


def build_order(messages):
    rate = {"x": 0.045, "y": 0.045, "z": 0.045, "c": 0.25}
    unit = CR * QC * 2 / 1e6
    rank = {"wt": -1, "by": 0, "az": 0, "bz": 1, "ay": 1}
    waiting = sorted(messages, key=lambda m: (m["k"], rank.get(m["name"][0], 2)))
    done = {("own", k) for k in range(CH)}
    order = [("own", k) for k in range(CH)]
    flying, free, now = [], {}, 0.0
    groups = range(SLOTS // GROUP)
    steps = [(("want",), {("wt", 0, d) for d in (1, -1, 2)})]
    for k in range(CH):
        gather = {m["name"] for m in messages if m["k"] == k and m["link"][0] != "x"}
        steps.append((("sel", k), gather | {("want",)}))
    steps.append((("queries",), set()))
    last = CH - 1
    for k in range(last):
        for g in groups:
            here = {m["name"] for m in messages if m["k"] == k and m.get("g") == g and m["name"][0] in ("xd", "xx")}
            steps.append((("kv", k, g), here | {("sel", k)}))
    final = {m["name"] for m in messages if m["k"] == last and m["name"][0] == "xd"}

    def launch():
        rest = []
        for m in waiting:
            at = free.get(m["link"], 0.0)
            if (at - now < LOOK or m["link"][0] == "x") and all(a in done for a in m["after"]):
                end = max(now, at) + m["size"] * unit / rate[m["link"][0]]
                free[m["link"]] = end
                if m["name"] not in final:
                    flying.append((end + 1.5, len(order), m))
                order.append(("start", m["name"]))
            else:
                rest.append(m)
        waiting[:] = rest

    launch()
    while flying or waiting or steps:
        flying.sort(key=lambda f: f[:2])
        ready = [step for step in steps if step[1] <= done]
        if ready and (ready[0][0][0] in ("sel", "want") or not flying or flying[0][0] > now + 0.3):
            name = ready[0][0]
            steps.remove(ready[0])
            order.append(name)
            now += COST[name[0]]
            done.add(name)
        elif flying:
            t, _, m = flying.pop(0)
            now = max(now, t) + 0.05
            order.append(("wait", m["name"]))
            done.add(m["name"])
        else:
            now += 0.5
        launch()
    order.append(("finish", [("xd", last, d, 0) for d in (1, -1)]))
    return order, now + sum(COST[c] for c in ("kv", "attend")) * len(groups)


MESSAGES = build_messages()
ORDER, MODELLED = build_order(MESSAGES)
NUMBER = {m["name"]: n for n, m in enumerate(MESSAGES)}
PER_GROUP = [6 if quads == 1 else 2 for quads in KINDS]


def wrap(value, size):
    return lax.rem(value + 2 * size, size)


def normed(rows, gain):
    rows = rows.astype(F32)
    centred = rows - jnp.mean(rows, axis=-1, keepdims=True)
    variance = jnp.mean(centred * centred, axis=-1, keepdims=True)
    return (centred * lax.rsqrt(variance + EPS) * gain).astype(BF)


PAIRS_OF_HEADS = HEADS // 2


def decode_kernel(tokens_ref, embed_weight_ref, gain_query_ref, gain_memory_ref, query_weight_hbm, key_weight_hbm,
                  value_weight_hbm, out_weight_hbm, pairs_ref, count_ref, decoded_ref, *scratch):
    gathered = scratch[:CH]
    (out_going, passing, memory, embedded, want_vmem, want, weights_vmem, stacked, rows, keys, values, context,
     send_sem, recv_sem, local_sem) = scratch[CH:]
    img = lax.axis_index("img")
    x = lax.axis_index("grp")
    y = img // (2 * NZ)
    z = lax.rem(img // 2, NZ)
    core = lax.rem(img, 2)

    def device(link):
        axis, d = link
        if axis == "x":
            return (img, wrap(x + d, NX))
        if axis == "y":
            return ((wrap(y + d, NY) * NZ + z) * 2 + core, x)
        if axis == "z":
            return ((y * NZ + wrap(z + d, NZ)) * 2 + core, x)
        return ((y * NZ + z) * 2 + (1 - core), x)

    barrier = pltpu.get_barrier_semaphore()
    partners = [("x", 1), ("x", -1), ("x", 2), ("y", 1), ("y", -1), ("z", 1), ("z", -1), ("c", 1)]
    for link in partners:
        pl.semaphore_signal(barrier, inc=1, device_id=device(link), device_id_type=MESH)

    loads = [pltpu.make_async_copy(hbm, weights_vmem.at[n], local_sem.at[n])
             for n, hbm in enumerate((query_weight_hbm, key_weight_hbm, value_weight_hbm, out_weight_hbm))]
    for load in loads:
        load.start()

    want_vmem[0] = jnp.zeros_like(want_vmem[0])
    want_vmem[0, :2, :SLOTS] = pairs_ref[...]
    for n in range(IMG):
        embedded[n] = jnp.dot(tokens_ref[n], embed_weight_ref[...], preferred_element_type=F32).astype(BF)

    pl.semaphore_wait(barrier, len(partners))

    def slice_of(m):
        def pick(where, at, size):
            return pl.ds(0, size) if where[0] == "all" else pl.ds(wrap(at + where[1], size), 1)

        first, count = m["l"]
        return gathered[m["k"]].at[pl.ds(0, KINDS[m["k"]]), core, pick(m["y"], y, NY), pick(m["z"], z, NZ),
                                   pl.ds(first, count)]

    def descriptor(name, step=0):
        n = NUMBER[name]
        m = MESSAGES[n]
        kind = name[0]
        half = GROUP // 2
        if kind == "wt":
            src = want_vmem.at[0]
            dst = want_vmem.at[(-m["d"]) % NX]
        elif kind in ("xd", "xf", "xx"):
            k, g, d = m["k"], m["g"] + step, m["d"]
            n = n + step * PER_GROUP[k]
            slots = pl.ds(g * GROUP, GROUP)
            some = pl.ds(g * GROUP + (0 if d == 1 else half), half)
            if kind == "xd":
                src = out_going.at[k, 0 if d == 1 else 1, slots]
                dst = memory.at[(-d) % NX, k, slots]
            elif kind == "xf":
                src = out_going.at[k, 2, some]
                dst = passing.at[some]
            else:
                src = passing.at[some]
                dst = memory.at[2, k, some]
        else:
            src = dst = slice_of(m)
        return pltpu.make_async_remote_copy(
            src_ref=src, dst_ref=dst, send_sem=send_sem.at[n], recv_sem=recv_sem.at[n],
            device_id=device(m["link"]), device_id_type=MESH)

    def place_own(k):
        for q in range(KINDS[k]):
            quadrant = wrap(x + 2 * q, 4)
            row = pl.multiple_of((quadrant // 2) * QR + k * CR, CR)
            column = pl.multiple_of(lax.rem(quadrant, 2) * QC, 128)
            for n in range(IMG):
                gathered[k][q, core, y, z, n] = embedded[n, pl.ds(row, CR), pl.ds(column, QC)]

    def read_wants():
        move = pltpu.make_async_copy(want_vmem, want, local_sem.at[4])
        move.start()
        move.wait()

    def select(k):
        def body(s, carry):
            def read(q, d):
                image = want[d % NX, 1, s]
                owner = image // IMG
                return gathered[k][q, lax.rem(owner, 2), owner // (2 * NZ), lax.rem(owner // 2, NZ),
                                   lax.rem(image, IMG)]

            out_going[k, 0, s] = read(0, 1)
            out_going[k, 1, s] = read(0, -1)
            if KINDS[k] == 1:
                out_going[k, 2, s] = read(0, 2)
            else:
                memory[2, k, s] = read(1, 0)
            memory[0, k, s] = read(0, 0)
            return carry

        lax.fori_loop(0, SLOTS, body, 0)

    lane = lax.broadcasted_iota(jnp.int32, (TOK, 2 * HEAD), 1)

    def make_queries():
        for load in loads:
            load.wait()

        def body(n, carry):
            query_rows = jnp.dot(normed(embedded[n], gain_query_ref[...]), weights_vmem[0],
                                 preferred_element_type=F32).astype(BF).astype(F32) * HEAD ** (-0.5)
            for p in range(PAIRS_OF_HEADS):
                both = query_rows[:, p * 2 * HEAD:(p + 1) * 2 * HEAD]
                stacked[n, p, :TOK] = jnp.where(lane < HEAD, both, 0.0).astype(BF)
                stacked[n, p, TOK:] = jnp.where(lane >= HEAD, both, 0.0).astype(BF)
            return carry

        lax.fori_loop(0, IMG, body, 0)

    def project(k, g):
        slots = pl.ds(g * GROUP, GROUP)
        for quadrant in range(4):
            part = memory[wrap(quadrant - x, 4), k, slots]
            rows[:, (quadrant // 2) * CR:(quadrant // 2 + 1) * CR, (quadrant % 2) * QC:(quadrant % 2 + 1) * QC] = part
        here = normed(rows[...].reshape(GROUP * 2 * CR, D_DEC), gain_memory_ref[...])
        for n, result in ((1, keys), (2, values)):
            made = jnp.dot(here, weights_vmem[n], preferred_element_type=F32).astype(BF)
            result[slots, 2 * CR * k:2 * CR * (k + 1)] = made.reshape(GROUP, 2 * CR, D_DEC)

    def attend(g):
        for b in range(GROUP):
            slot = g * GROUP + b
            image = lax.rem(want[0, 0, slot], IMG)
            for p in range(PAIRS_OF_HEADS):
                columns = slice(p * 2 * HEAD, (p + 1) * 2 * HEAD)
                scores = lax.dot_general(stacked[image, p], keys[slot, :, columns], (((1,), (1,)), ((), ())),
                                         preferred_element_type=F32)
                powers = jnp.exp(scores - jnp.max(scores, axis=-1, keepdims=True))
                share = 1.0 / jnp.sum(powers, axis=-1, keepdims=True)
                mixed = jnp.dot((powers * share).astype(BF), values[slot, :, columns], preferred_element_type=F32)
                context[b * TOK:(b + 1) * TOK, columns] = jnp.where(
                    lane < HEAD, mixed[:TOK], mixed[TOK:]).astype(BF)
        projected = jnp.dot(context[...], weights_vmem[3], preferred_element_type=F32)
        for b in range(GROUP):
            slot = g * GROUP + b
            image = lax.rem(want[0, 0, slot], IMG)
            combined = embedded[image].astype(F32) + projected[b * TOK:(b + 1) * TOK]
            decoded_ref[slot] = jnp.where(slot < count_ref[0], combined, 0.0).astype(BF)

    def finish(names):
        def body(g, carry):
            for name in names:
                descriptor(name, g).wait_recv()
            project(CH - 1, g)
            attend(g)
            return carry

        lax.fori_loop(0, SLOTS // GROUP, body, 0)

    run = dict(own=place_own, want=read_wants, sel=select, queries=make_queries, kv=project,
               finish=finish,
               start=lambda name: descriptor(name).start(), wait=lambda name: descriptor(name).wait_recv())
    for what, *which in ORDER:
        run[what](*which)
    for m in MESSAGES:
        descriptor(m["name"]).wait_send()


def decode(tokens, embed_weight, gain_query, gain_memory, query_weight, key_weight, value_weight, out_weight, pairs,
           counts):
    vmem = pl.BlockSpec(memory_space=pltpu.VMEM)
    hbm = pl.BlockSpec(memory_space=pl.ANY)
    return pl.pallas_call(
        decode_kernel,
        out_shape=pltpu.VMEM((SLOTS, TOK, D_DEC), BF),
        in_specs=[vmem, vmem, vmem, vmem, hbm, hbm, hbm, hbm, vmem, pl.BlockSpec(memory_space=pltpu.SMEM)],
        out_specs=vmem,
        scratch_shapes=[
            *(pltpu.VMEM((quads, 2, NY, NZ, IMG, CR, QC), BF) for quads in KINDS),
            pltpu.VMEM((CH, 3, SLOTS, CR, QC), BF),
            pltpu.VMEM((SLOTS, CR, QC), BF),
            pltpu.VMEM((4, CH, SLOTS, CR, QC), BF),
            pltpu.VMEM((IMG, TOK, D_DEC), BF),
            pltpu.VMEM((NX, 8, 128), jnp.int32),
            pltpu.SMEM((NX, 8, 128), jnp.int32),
            pltpu.VMEM((4, D_DEC, D_DEC), BF),
            pltpu.VMEM((IMG, PAIRS_OF_HEADS, 2 * TOK, 2 * HEAD), BF),
            pltpu.VMEM((GROUP, 2 * CR, D_DEC), BF),
            pltpu.VMEM((SLOTS, TOK, D_DEC), BF),
            pltpu.VMEM((SLOTS, TOK, D_DEC), BF),
            pltpu.VMEM((GROUP * TOK, D_DEC), BF),
            pltpu.SemaphoreType.DMA((len(MESSAGES),)),
            pltpu.SemaphoreType.DMA((len(MESSAGES),)),
            pltpu.SemaphoreType.DMA((5,)),
        ],
        compiler_params=pltpu.CompilerParams(
            collective_id=0, has_side_effects=True, vmem_limit_bytes=57 * 1024 * 1024
        ),
        name="decode",
    )(tokens, embed_weight, gain_query, gain_memory, query_weight, key_weight, value_weight, out_weight, pairs, counts)


def on_device(
    tokens,
    embed_weight,
    gain_query,
    gain_memory,
    query_weight,
    key_weight,
    value_weight,
    out_weight,
    pair_list,
    counts,
):
    return decode(tokens, embed_weight, gain_query, gain_memory, query_weight, key_weight, value_weight, out_weight,
                  pair_list.T, counts)


def solution(mesh):
    placed = (
        P("img", None, None),
        P(),
        P(),
        P(),
        P(),
        P(),
        P(),
        P(),
        P(("img", "grp"), None),
        P(("img", "grp")),
    )
    return jax.shard_map(
        on_device,
        mesh=mesh,
        in_specs=placed,
        out_specs=P(("img", "grp"), None, None),
        check_vma=False,
    )
```

```python
import functools

import jax
import jax.numpy as jnp
from jax import lax
from jax.experimental import pallas as pl
from jax.experimental.pallas import tpu as pltpu
from jax.sharding import PartitionSpec as P

HEADS = 12
HEAD = 64
D_DEC = 768
D_ENC = 1024
TOK = 96
IMG = 4
SLOTS = 36
EPS = 1e-06

QR = TOK // 2
QC = D_DEC // 2
CH = 3
CR = QR // CH
KINDS = (1, 2, 2)
GROUP = 12

NY, NZ, NX = 4, 8, 4
MESH = pl.DeviceIdType.MESH
BF = jnp.bfloat16
F32 = jnp.float32


def build_messages():
    messages = []
    for d in (1, -1, 2):
        messages.append(dict(name=("wt", 0, d), link=("x", d), size=0.5, after=(), k=0, d=d))

    def add(name, link, size, after, **where):
        messages.append(dict(name=name, link=link, size=size, after=tuple(after), k=name[1], **where))

    hz, hy = NZ // 2, NY // 2

    def part(first, far, d):
        return (first, 2) if not far else (first + (d == -1), 1)

    for k in range(CH):
        quads = KINDS[k]
        own = ("own", k)
        along_z, along_y = {0: [own]}, {0: [own]}
        for s in range(1, hz + 1):
            for d in (1, -1):
                name, images = ("az", k, d, s), part(0, s == hz, d)
                add(name, ("z", d), quads * images[1], [("az", k, d, s - 1)] if s > 1 else [own],
                    y=("one", 0), z=("one", -d * (s - 1)), l=images)
                along_z.setdefault(hz if s == hz else -d * s, []).append(name)
        for s in range(1, hy + 1):
            for d in (1, -1):
                name, images = ("by", k, d, s), part(2, s == hy, d)
                add(name, ("y", d), quads * images[1], [("by", k, d, s - 1)] if s > 1 else [own],
                    y=("one", -d * (s - 1)), z=("one", 0), l=images)
                along_y.setdefault(hy if s == hy else -d * s, []).append(name)
        columns, planes = {}, {}
        for s in range(1, hy + 1):
            for d in (1, -1):
                images = part(0, s == hy, d)
                for at, arrived in along_z.items():
                    name = ("ay", k, d, s, at)
                    add(name, ("y", d), quads * images[1], [("ay", k, d, s - 1, at)] if s > 1 else arrived,
                        y=("one", -d * (s - 1)), z=("one", at), l=images)
                    columns.setdefault(hy if s == hy else -d * s, []).append(name)
        for s in range(1, hz + 1):
            for d in (1, -1):
                images = part(2, s == hz, d)
                for at, arrived in along_y.items():
                    name = ("bz", k, d, s, at)
                    add(name, ("z", d), quads * images[1], [("bz", k, d, s - 1, at)] if s > 1 else arrived,
                        y=("one", at), z=("one", -d * (s - 1)), l=images)
                    planes.setdefault(hz if s == hz else -d * s, []).append(name)
        columns[0] = [n for at in along_z.values() for n in at]
        planes[0] = [n for at in along_y.values() for n in at]
        for at, arrived in columns.items():
            add(("sa", k, at), ("c", 1), quads * 2 * NZ, arrived, y=("one", at), z=("all",), l=(0, 2))
        for at, arrived in planes.items():
            add(("sb", k, at), ("c", 1), quads * 2 * NY, arrived, y=("all",), z=("one", at), l=(2, 2))
        for g in range(SLOTS // GROUP):
            for d in (1, -1):
                if quads == 1:
                    add(("xf", k, d, g), ("x", d), GROUP // 2, [("sel", k)], g=g, d=d)
            for d in (1, -1):
                add(("xd", k, d, g), ("x", d), GROUP, [("sel", k)], g=g, d=d)
            if quads == 1:
                for d in (1, -1):
                    add(("xx", k, d, g), ("x", d), GROUP // 2, [("xf", k, d, g)], g=g, d=d)
    return messages


LOOK = 2.0
LOOK_X = 2.5
COST = {"sel": 1.0, "queries": 1.5, "kv": 1.2, "attend": 6.0, "want": 0.5}
EVENTS = 8


def build_order(messages):
    rate = {"x": 0.045, "y": 0.045, "z": 0.045, "c": 0.25}
    unit = CR * QC * 2 / 1e6
    rank = {"wt": -1, "by": 0, "az": 0, "bz": 1, "ay": 1}
    waiting = sorted(messages, key=lambda m: (m["k"], rank.get(m["name"][0], 2)))
    done = {("own", k) for k in range(CH)}
    order = [("own", k) for k in range(CH)]
    flying, free, now, since = [], {}, 0.0, 0
    groups = range(SLOTS // GROUP)
    steps = [(("want",), {("wt", 0, d) for d in (1, -1, 2)})]
    for k in range(CH):
        gather = {m["name"] for m in messages if m["k"] == k and m["link"][0] != "x"}
        steps.append((("sel", k), gather | {("want",)}))
    steps.append((("queries",), set()))
    last = CH - 1
    for k in range(last):
        for g in groups:
            here = {m["name"] for m in messages if m["k"] == k and m.get("g") == g and m["name"][0] in ("xd", "xx")}
            steps.append((("kv", k, g), here | {("sel", k)}))
    final = {m["name"] for m in messages if m["k"] == last and m["name"][0] == "xd"}

    def launch():
        rest = []
        for m in waiting:
            at = free.get(m["link"], 0.0)
            look = LOOK if m["link"][0] != "x" else 1e3 if ("sel", last) in done else LOOK_X
            if at - now < look and all(a in done for a in m["after"]):
                end = max(now, at) + m["size"] * unit / rate[m["link"][0]]
                free[m["link"]] = end
                if m["name"] not in final:
                    flying.append((end + 1.5, len(order), m))
                order.append(("start", m["name"]))
            else:
                rest.append(m)
        waiting[:] = rest

    launch()
    while flying or waiting or steps:
        flying.sort(key=lambda f: f[:2])
        ready = [step for step in steps if step[1] <= done]
        ready.sort(key=lambda step: step[0][0] not in ("sel", "want"))
        if ready and (ready[0][0][0] in ("sel", "want") or not flying or flying[0][0] > now + 0.3 or since >= EVENTS):
            name = ready[0][0]
            steps.remove(ready[0])
            order.append(name)
            now += COST[name[0]]
            done.add(name)
            since = 0
            if name == ("sel", last):
                launch()
                order.append(("drain",))
        elif flying:
            t, _, m = flying.pop(0)
            now = max(now, t) + 0.1
            since += 1
            order.append(("wait", m["name"]))
            done.add(m["name"])
        else:
            now += 0.5
        launch()
    order.append(("finish", [("xd", last, d, 0) for d in (1, -1)]))
    return order, now + sum(COST[c] for c in ("kv", "attend")) * len(groups)


MESSAGES = build_messages()
ORDER, MODELLED = build_order(MESSAGES)
NUMBER = {m["name"]: n for n, m in enumerate(MESSAGES)}
PER_GROUP = [6 if quads == 1 else 2 for quads in KINDS]


def wrap(value, size):
    return lax.rem(value + 2 * size, size)


def normed(rows, gain):
    rows = rows.astype(F32)
    centred = rows - jnp.mean(rows, axis=-1, keepdims=True)
    variance = jnp.mean(centred * centred, axis=-1, keepdims=True)
    return (centred * lax.rsqrt(variance + EPS) * gain).astype(BF)


PAIRS_OF_HEADS = HEADS // 2


def decode_kernel(tokens_ref, embed_weight_ref, gain_query_ref, gain_memory_ref, query_weight_hbm, key_weight_hbm,
                  value_weight_hbm, out_weight_hbm, pairs_ref, count_ref, decoded_ref, *scratch):
    gathered = scratch[:CH]
    (out_going, passing, memory, embedded, want_vmem, want, weights_vmem, stacked, rows, keys, values, context,
     send_sem, recv_sem, local_sem) = scratch[CH:]
    img = lax.axis_index("img")
    x = lax.axis_index("grp")
    y = img // (2 * NZ)
    z = lax.rem(img // 2, NZ)
    core = lax.rem(img, 2)

    def device(link):
        axis, d = link
        if axis == "x":
            return (img, wrap(x + d, NX))
        if axis == "y":
            return ((wrap(y + d, NY) * NZ + z) * 2 + core, x)
        if axis == "z":
            return ((y * NZ + wrap(z + d, NZ)) * 2 + core, x)
        return ((y * NZ + z) * 2 + (1 - core), x)

    barrier = pltpu.get_barrier_semaphore()
    partners = [("x", 1), ("x", -1), ("x", 2), ("y", 1), ("y", -1), ("z", 1), ("z", -1), ("c", 1)]
    for link in partners:
        pl.semaphore_signal(barrier, inc=1, device_id=device(link), device_id_type=MESH)

    loads = [pltpu.make_async_copy(hbm, weights_vmem.at[n], local_sem.at[n])
             for n, hbm in enumerate((query_weight_hbm, key_weight_hbm, value_weight_hbm, out_weight_hbm))]
    for load in loads:
        load.start()

    want_vmem[0] = jnp.zeros_like(want_vmem[0])
    want_vmem[0, :2, :SLOTS] = pairs_ref[...]
    embedded[...] = jnp.dot(tokens_ref[...].reshape(IMG * TOK, D_ENC), embed_weight_ref[...],
                            preferred_element_type=F32).astype(BF).reshape(IMG, TOK, D_DEC)

    pl.semaphore_wait(barrier, len(partners))

    def slice_of(m):
        def pick(where, at, size):
            return pl.ds(0, size) if where[0] == "all" else pl.ds(wrap(at + where[1], size), 1)

        first, count = m["l"]
        return gathered[m["k"]].at[pl.ds(0, KINDS[m["k"]]), core, pick(m["y"], y, NY), pick(m["z"], z, NZ),
                                   pl.ds(first, count)]

    def descriptor(name, step=0):
        n = NUMBER[name]
        m = MESSAGES[n]
        kind = name[0]
        half = GROUP // 2
        if kind == "wt":
            src = want_vmem.at[0]
            dst = want_vmem.at[(-m["d"]) % NX]
        elif kind in ("xd", "xf", "xx"):
            k, g, d = m["k"], m["g"] + step, m["d"]
            n = n + step * PER_GROUP[k]
            slots = pl.ds(g * GROUP, GROUP)
            some = pl.ds(g * GROUP + (0 if d == 1 else half), half)
            if kind == "xd":
                src = out_going.at[k, 0 if d == 1 else 1, slots]
                dst = memory.at[(-d) % NX, k, slots]
            elif kind == "xf":
                src = out_going.at[k, 2, some]
                dst = passing.at[some]
            else:
                src = passing.at[some]
                dst = memory.at[2, k, some]
        else:
            src = dst = slice_of(m)
        return pltpu.make_async_remote_copy(
            src_ref=src, dst_ref=dst, send_sem=send_sem.at[n], recv_sem=recv_sem.at[n],
            device_id=device(m["link"]), device_id_type=MESH)

    def place_own(k):
        for q in range(KINDS[k]):
            quadrant = wrap(x + 2 * q, 4)
            row = pl.multiple_of((quadrant // 2) * QR + k * CR, CR)
            column = pl.multiple_of(lax.rem(quadrant, 2) * QC, 128)
            for n in range(IMG):
                gathered[k][q, core, y, z, n] = embedded[n, pl.ds(row, CR), pl.ds(column, QC)]

    def read_wants():
        move = pltpu.make_async_copy(want_vmem, want, local_sem.at[4])
        move.start()
        move.wait()

    def select(k):
        def body(s, carry):
            def read(q, d):
                image = want[d % NX, 1, s]
                owner = image // IMG
                return gathered[k][q, lax.rem(owner, 2), owner // (2 * NZ), lax.rem(owner // 2, NZ),
                                   lax.rem(image, IMG)]

            out_going[k, 0, s] = read(0, 1)
            out_going[k, 1, s] = read(0, -1)
            if KINDS[k] == 1:
                out_going[k, 2, s] = read(0, 2)
            else:
                memory[2, k, s] = read(1, 0)
            memory[0, k, s] = read(0, 0)
            return carry

        lax.fori_loop(0, SLOTS, body, 0)

    lane = lax.broadcasted_iota(jnp.int32, (TOK, 2 * HEAD), 1)

    def make_queries():
        for load in loads:
            load.wait()

        query_rows = jnp.dot(normed(embedded[...].reshape(IMG * TOK, D_DEC), gain_query_ref[...]), weights_vmem[0],
                             preferred_element_type=F32).astype(BF).astype(F32) * HEAD ** (-0.5)
        for n in range(IMG):
            for p in range(PAIRS_OF_HEADS):
                both = query_rows[n * TOK:(n + 1) * TOK, p * 2 * HEAD:(p + 1) * 2 * HEAD]
                stacked[n, p, :TOK] = jnp.where(lane < HEAD, both, 0.0).astype(BF)
                stacked[n, p, TOK:] = jnp.where(lane >= HEAD, both, 0.0).astype(BF)

    def project(k, g):
        slots = pl.ds(g * GROUP, GROUP)
        for quadrant in range(4):
            part = memory[wrap(quadrant - x, 4), k, slots]
            rows[:, (quadrant // 2) * CR:(quadrant // 2 + 1) * CR, (quadrant % 2) * QC:(quadrant % 2 + 1) * QC] = part
        here = normed(rows[...].reshape(GROUP * 2 * CR, D_DEC), gain_memory_ref[...])
        for n, result in ((1, keys), (2, values)):
            made = jnp.dot(here, weights_vmem[n], preferred_element_type=F32).astype(BF)
            result[slots, 2 * CR * k:2 * CR * (k + 1)] = made.reshape(GROUP, 2 * CR, D_DEC)

    def attend(g):
        for b in range(GROUP):
            slot = g * GROUP + b
            image = lax.rem(want[0, 0, slot], IMG)
            for p in range(PAIRS_OF_HEADS):
                columns = slice(p * 2 * HEAD, (p + 1) * 2 * HEAD)
                scores = lax.dot_general(stacked[image, p], keys[slot, :, columns], (((1,), (1,)), ((), ())),
                                         preferred_element_type=F32)
                powers = jnp.exp(scores - jnp.max(scores, axis=-1, keepdims=True))
                share = 1.0 / jnp.sum(powers, axis=-1, keepdims=True)
                mixed = jnp.dot((powers * share).astype(BF), values[slot, :, columns], preferred_element_type=F32)
                context[b * TOK:(b + 1) * TOK, columns] = jnp.where(
                    lane < HEAD, mixed[:TOK], mixed[TOK:]).astype(BF)
        projected = jnp.dot(context[...], weights_vmem[3], preferred_element_type=F32)
        for b in range(GROUP):
            slot = g * GROUP + b
            image = lax.rem(want[0, 0, slot], IMG)
            combined = embedded[image].astype(F32) + projected[b * TOK:(b + 1) * TOK]
            decoded_ref[slot] = jnp.where(slot < count_ref[0], combined, 0.0).astype(BF)

    def drain():
        for m in MESSAGES:
            if m["link"][0] != "x":
                descriptor(m["name"]).wait_send()

    def finish(names):
        def body(g, carry):
            for name in names:
                descriptor(name, g).wait_recv()
            project(CH - 1, g)
            attend(g)
            return carry

        lax.fori_loop(0, SLOTS // GROUP, body, 0)

    run = dict(own=place_own, want=read_wants, sel=select, queries=make_queries, kv=project,
               finish=finish, drain=drain,
               start=lambda name: descriptor(name).start(), wait=lambda name: descriptor(name).wait_recv())
    for what, *which in ORDER:
        run[what](*which)
    for m in MESSAGES:
        if m["link"][0] == "x":
            descriptor(m["name"]).wait_send()


def decode(tokens, embed_weight, gain_query, gain_memory, query_weight, key_weight, value_weight, out_weight, pairs,
           counts):
    vmem = pl.BlockSpec(memory_space=pltpu.VMEM)
    hbm = pl.BlockSpec(memory_space=pl.ANY)
    return pl.pallas_call(
        decode_kernel,
        out_shape=pltpu.VMEM((SLOTS, TOK, D_DEC), BF),
        in_specs=[vmem, vmem, vmem, vmem, hbm, hbm, hbm, hbm, vmem, pl.BlockSpec(memory_space=pltpu.SMEM)],
        out_specs=vmem,
        scratch_shapes=[
            *(pltpu.VMEM((quads, 2, NY, NZ, IMG, CR, QC), BF) for quads in KINDS),
            pltpu.VMEM((CH, 3, SLOTS, CR, QC), BF),
            pltpu.VMEM((SLOTS, CR, QC), BF),
            pltpu.VMEM((4, CH, SLOTS, CR, QC), BF),
            pltpu.VMEM((IMG, TOK, D_DEC), BF),
            pltpu.VMEM((NX, 8, 128), jnp.int32),
            pltpu.SMEM((NX, 8, 128), jnp.int32),
            pltpu.VMEM((4, D_DEC, D_DEC), BF),
            pltpu.VMEM((IMG, PAIRS_OF_HEADS, 2 * TOK, 2 * HEAD), BF),
            pltpu.VMEM((GROUP, 2 * CR, D_DEC), BF),
            pltpu.VMEM((SLOTS, TOK, D_DEC), BF),
            pltpu.VMEM((SLOTS, TOK, D_DEC), BF),
            pltpu.VMEM((GROUP * TOK, D_DEC), BF),
            pltpu.SemaphoreType.DMA((len(MESSAGES),)),
            pltpu.SemaphoreType.DMA((len(MESSAGES),)),
            pltpu.SemaphoreType.DMA((5,)),
        ],
        compiler_params=pltpu.CompilerParams(
            collective_id=0, has_side_effects=True, vmem_limit_bytes=57 * 1024 * 1024
        ),
        name="decode",
    )(tokens, embed_weight, gain_query, gain_memory, query_weight, key_weight, value_weight, out_weight, pairs, counts)


def on_device(
    tokens,
    embed_weight,
    gain_query,
    gain_memory,
    query_weight,
    key_weight,
    value_weight,
    out_weight,
    pair_list,
    counts,
):
    return decode(tokens, embed_weight, gain_query, gain_memory, query_weight, key_weight, value_weight, out_weight,
                  pair_list.T, counts)


def solution(mesh):
    placed = (
        P("img", None, None),
        P(),
        P(),
        P(),
        P(),
        P(),
        P(),
        P(),
        P(("img", "grp"), None),
        P(("img", "grp")),
    )
    return jax.shard_map(
        on_device,
        mesh=mesh,
        in_specs=placed,
        out_specs=P(("img", "grp"), None, None),
        check_vma=False,
    )
```

```python
import functools

import jax
import jax.numpy as jnp
from jax import lax
from jax.experimental import pallas as pl
from jax.experimental.pallas import tpu as pltpu
from jax.sharding import PartitionSpec as P

HEADS = 12
HEAD = 64
D_DEC = 768
D_ENC = 1024
TOK = 96
IMG = 4
SLOTS = 36
EPS = 1e-06

QR = TOK // 2
QC = D_DEC // 2
CH = 3
CR = QR // CH
KINDS = (1, 2, 2)
EARLY = (3, 2, 2)
FINE_Y = (True, True, False)
FINE_Z = (False, False, False)
GROUP = 12

NY, NZ, NX = 4, 8, 4
MESH = pl.DeviceIdType.MESH
BF = jnp.bfloat16
F32 = jnp.float32


def build_messages():
    messages = []
    for d in (1, -1, 2):
        messages.append(dict(name=("wt", 0, d), link=("x", d), size=0.5, after=(), k=0, d=d))

    def add(name, link, size, after, **where):
        messages.append(dict(name=name, link=link, size=size, after=tuple(after), k=name[1], **where))

    hz, hy = NZ // 2, NY // 2

    def part(first, count, far, d):
        if not far:
            return (first, count)
        upper = (count + 1) // 2
        return (first, upper) if d == 1 else (first + upper, count - upper)

    def all_of(legs, fine):
        return legs if fine else {"all": [n for names in legs.values() for n in names]}

    for k in range(CH):
        quads = KINDS[k]
        own = ("own", k)
        early = EARLY[k]
        along_z, along_y = {0: [own]}, {0: [own]}
        for s in range(1, hz + 1):
            for d in (1, -1):
                name, images = ("az", k, d, s), part(0, early, s == hz, d)
                if images[1]:
                    add(name, ("z", d), quads * images[1], [("az", k, d, s - 1)] if s > 1 else [own],
                        y=("one", 0), z=("one", -d * (s - 1)), l=images)
                    along_z.setdefault(hz if s == hz else -d * s, []).append(name)
        for s in range(1, hy + 1):
            for d in (1, -1):
                name, images = ("by", k, d, s), part(early, IMG - early, s == hy, d)
                if images[1]:
                    add(name, ("y", d), quads * images[1], [("by", k, d, s - 1)] if s > 1 else [own],
                        y=("one", -d * (s - 1)), z=("one", 0), l=images)
                    along_y.setdefault(hy if s == hy else -d * s, []).append(name)
        columns, planes = {}, {}
        for s in range(1, hy + 1):
            for d in (1, -1):
                images = part(0, early, s == hy, d)
                for at, arrived in all_of(along_z, FINE_Y[k]).items():
                    name = ("ay", k, d, s, at)
                    if images[1]:
                        add(name, ("y", d), quads * images[1] * (NZ if at == "all" else 1),
                            [("ay", k, d, s - 1, at)] if s > 1 else arrived,
                            y=("one", -d * (s - 1)), z=("all",) if at == "all" else ("one", at), l=images)
                        columns.setdefault(hy if s == hy else -d * s, []).append(name)
        for s in range(1, hz + 1):
            for d in (1, -1):
                images = part(early, IMG - early, s == hz, d)
                for at, arrived in all_of(along_y, FINE_Z[k]).items():
                    name = ("bz", k, d, s, at)
                    if images[1]:
                        add(name, ("z", d), quads * images[1] * (NY if at == "all" else 1),
                            [("bz", k, d, s - 1, at)] if s > 1 else arrived,
                            y=("all",) if at == "all" else ("one", at), z=("one", -d * (s - 1)), l=images)
                        planes.setdefault(hz if s == hz else -d * s, []).append(name)
        columns[0] = [n for at in along_z.values() for n in at]
        planes[0] = [n for at in along_y.values() for n in at]
        for at, arrived in columns.items():
            add(("sa", k, at), ("c", 1), quads * early * NZ, arrived, y=("one", at), z=("all",), l=(0, early))
        for at, arrived in planes.items():
            add(("sb", k, at), ("c", 1), quads * (IMG - early) * NY, arrived, y=("all",), z=("one", at),
                l=(early, IMG - early))
        for g in range(SLOTS // GROUP):
            for d in (1, -1):
                if quads == 1:
                    add(("xf", k, d, g), ("x", d), GROUP // 2, [("sel", k)], g=g, d=d)
            for d in (1, -1):
                add(("xd", k, d, g), ("x", d), GROUP, [("sel", k)], g=g, d=d)
            if quads == 1:
                for d in (1, -1):
                    add(("xx", k, d, g), ("x", d), GROUP // 2, [("xf", k, d, g)], g=g, d=d)
    return messages


LOOK = 3.0
LOOK_X = 2.5
COST = {"sel": 1.0, "queries": 1.5, "kv": 1.2, "attend": 6.0, "want": 0.5}
EVENTS = 8


def with_drains(order, names, behind=48):
    result, started = [], []
    for n, entry in enumerate(order):
        result.append(entry)
        if entry[0] == "start" and entry[1] in names:
            started.append((n, entry[1]))
        elif entry[0] == "wait" and started and started[0][0] <= n - behind:
            result.append(("sent", started.pop(0)[1]))
        elif entry[0] == "drain":
            result.pop()
            result.extend(("sent", name) for _, name in started)
            started = []
    assert not started
    return result


def build_order(messages):
    rate = {"x": 0.055, "y": 0.045, "z": 0.045, "c": 0.25}
    unit = CR * QC * 2 / 1e6
    rank = {"wt": -1, "by": 0, "az": 0, "bz": 1, "ay": 1}
    waiting = sorted(messages, key=lambda m: (m["k"], rank.get(m["name"][0], 2)))
    done = {("own", k) for k in range(CH)}
    order = [("own", k) for k in range(CH)]
    flying, free, now, since = [], {}, 0.0, 0
    groups = range(SLOTS // GROUP)
    steps = [(("want",), {("wt", 0, d) for d in (1, -1, 2)})]
    for k in range(CH):
        gather = {m["name"] for m in messages if m["k"] == k and m["link"][0] != "x"}
        steps.append((("sel", k), gather | {("want",)}))
    steps.append((("queries",), set()))
    last = CH - 1
    for k in range(last):
        for g in groups:
            here = {m["name"] for m in messages if m["k"] == k and m.get("g") == g and m["name"][0] in ("xd", "xx")}
            steps.append((("kv", k, g), here | {("sel", k)}))
    final = {m["name"] for m in messages if m["k"] == last and m["name"][0] == "xd"}

    def launch():
        rest = []
        for m in waiting:
            at = free.get(m["link"], 0.0)
            look = LOOK if m["link"][0] != "x" else 1e3 if ("sel", last) in done else LOOK_X
            if at - now < look and all(a in done for a in m["after"]):
                end = max(now, at) + m["size"] * unit / rate[m["link"][0]]
                free[m["link"]] = end
                if m["name"] not in final:
                    flying.append((end + 1.5, len(order), m))
                order.append(("start", m["name"]))
            else:
                rest.append(m)
        waiting[:] = rest

    launch()
    while flying or waiting or steps:
        flying.sort(key=lambda f: f[:2])
        ready = [step for step in steps if step[1] <= done]
        ready.sort(key=lambda step: step[0][0] not in ("sel", "want"))
        if ready and (ready[0][0][0] in ("sel", "want") or not flying or flying[0][0] > now + 0.3 or since >= EVENTS):
            name = ready[0][0]
            steps.remove(ready[0])
            order.append(name)
            now += COST[name[0]]
            done.add(name)
            since = 0
            if name == ("sel", last):
                launch()
                order.append(("drain",))
        elif flying:
            t, _, m = flying.pop(0)
            now = max(now, t) + 0.15
            since += 1
            order.append(("wait", m["name"]))
            done.add(m["name"])
        else:
            now += 0.5
        launch()
    order.append(("finish", [("xd", last, d, 0) for d in (1, -1)]))
    order = with_drains(order, {m["name"] for m in messages if m["link"][0] != "x"})
    return order, now + sum(COST[c] for c in ("kv", "attend")) * len(groups)


MESSAGES = build_messages()
ORDER, MODELLED = build_order(MESSAGES)
NUMBER = {m["name"]: n for n, m in enumerate(MESSAGES)}
PER_GROUP = [6 if quads == 1 else 2 for quads in KINDS]


def wrap(value, size):
    return lax.rem(value + 2 * size, size)


def normed(rows, gain):
    rows = rows.astype(F32)
    centred = rows - jnp.mean(rows, axis=-1, keepdims=True)
    variance = jnp.mean(centred * centred, axis=-1, keepdims=True)
    return (centred * lax.rsqrt(variance + EPS) * gain).astype(BF)


PAIRS_OF_HEADS = HEADS // 2


def decode_kernel(tokens_ref, embed_weight_ref, gain_query_ref, gain_memory_ref, query_weight_hbm, key_weight_hbm,
                  value_weight_hbm, out_weight_hbm, pairs_ref, count_ref, decoded_ref, *scratch):
    gathered = scratch[:CH]
    (out_going, passing, memory, embedded, want_vmem, want, weights_vmem, stacked, rows, keys, values, context,
     send_sem, recv_sem, local_sem) = scratch[CH:]
    img = lax.axis_index("img")
    x = lax.axis_index("grp")
    y = img // (2 * NZ)
    z = lax.rem(img // 2, NZ)
    core = lax.rem(img, 2)

    def device(link):
        axis, d = link
        if axis == "x":
            return (img, wrap(x + d, NX))
        if axis == "y":
            return ((wrap(y + d, NY) * NZ + z) * 2 + core, x)
        if axis == "z":
            return ((y * NZ + wrap(z + d, NZ)) * 2 + core, x)
        return ((y * NZ + z) * 2 + (1 - core), x)

    barrier = pltpu.get_barrier_semaphore()
    partners = [("x", 1), ("x", -1), ("x", 2), ("y", 1), ("y", -1), ("z", 1), ("z", -1), ("c", 1)]
    for link in partners:
        pl.semaphore_signal(barrier, inc=1, device_id=device(link), device_id_type=MESH)

    loads = [pltpu.make_async_copy(hbm, weights_vmem.at[n], local_sem.at[n])
             for n, hbm in enumerate((query_weight_hbm, key_weight_hbm, value_weight_hbm, out_weight_hbm))]
    for load in loads:
        load.start()

    want_vmem[0] = jnp.zeros_like(want_vmem[0])
    want_vmem[0, :2, :SLOTS] = pairs_ref[...]
    embedded[...] = jnp.dot(tokens_ref[...].reshape(IMG * TOK, D_ENC), embed_weight_ref[...],
                            preferred_element_type=F32).astype(BF).reshape(IMG, TOK, D_DEC)

    pl.semaphore_wait(barrier, len(partners))

    def slice_of(m):
        def pick(where, at, size):
            return pl.ds(0, size) if where[0] == "all" else pl.ds(wrap(at + where[1], size), 1)

        first, count = m["l"]
        return gathered[m["k"]].at[pl.ds(0, KINDS[m["k"]]), core, pick(m["y"], y, NY), pick(m["z"], z, NZ),
                                   pl.ds(first, count)]

    def descriptor(name, step=0):
        n = NUMBER[name]
        m = MESSAGES[n]
        kind = name[0]
        half = GROUP // 2
        if kind == "wt":
            src = want_vmem.at[0]
            dst = want_vmem.at[(-m["d"]) % NX]
        elif kind in ("xd", "xf", "xx"):
            k, g, d = m["k"], m["g"] + step, m["d"]
            n = n + step * PER_GROUP[k]
            slots = pl.ds(g * GROUP, GROUP)
            some = pl.ds(g * GROUP + (0 if d == 1 else half), half)
            if kind == "xd":
                src = out_going.at[k, 0 if d == 1 else 1, slots]
                dst = memory.at[(-d) % NX, k, slots]
            elif kind == "xf":
                src = out_going.at[k, 2, some]
                dst = passing.at[some]
            else:
                src = passing.at[some]
                dst = memory.at[2, k, some]
        else:
            src = dst = slice_of(m)
        return pltpu.make_async_remote_copy(
            src_ref=src, dst_ref=dst, send_sem=send_sem.at[n], recv_sem=recv_sem.at[n],
            device_id=device(m["link"]), device_id_type=MESH)

    def place_own(k):
        for q in range(KINDS[k]):
            quadrant = wrap(x + 2 * q, 4)
            row = pl.multiple_of((quadrant // 2) * QR + k * CR, CR)
            column = pl.multiple_of(lax.rem(quadrant, 2) * QC, 128)
            for n in range(IMG):
                gathered[k][q, core, y, z, n] = embedded[n, pl.ds(row, CR), pl.ds(column, QC)]

    def read_wants():
        move = pltpu.make_async_copy(want_vmem, want, local_sem.at[4])
        move.start()
        move.wait()

    def select(k):
        def body(s, carry):
            def read(q, d):
                image = want[d % NX, 1, s]
                owner = image // IMG
                return gathered[k][q, lax.rem(owner, 2), owner // (2 * NZ), lax.rem(owner // 2, NZ),
                                   lax.rem(image, IMG)]

            out_going[k, 0, s] = read(0, 1)
            out_going[k, 1, s] = read(0, -1)
            if KINDS[k] == 1:
                out_going[k, 2, s] = read(0, 2)
            else:
                memory[2, k, s] = read(1, 0)
            memory[0, k, s] = read(0, 0)
            return carry

        lax.fori_loop(0, SLOTS, body, 0)

    lane = lax.broadcasted_iota(jnp.int32, (TOK, 2 * HEAD), 1)

    def make_queries():
        for load in loads:
            load.wait()

        query_rows = jnp.dot(normed(embedded[...].reshape(IMG * TOK, D_DEC), gain_query_ref[...]), weights_vmem[0],
                             preferred_element_type=F32).astype(BF).astype(F32) * HEAD ** (-0.5)
        for n in range(IMG):
            for p in range(PAIRS_OF_HEADS):
                both = query_rows[n * TOK:(n + 1) * TOK, p * 2 * HEAD:(p + 1) * 2 * HEAD]
                stacked[n, p, :TOK] = jnp.where(lane < HEAD, both, 0.0).astype(BF)
                stacked[n, p, TOK:] = jnp.where(lane >= HEAD, both, 0.0).astype(BF)

    def project(k, g):
        slots = pl.ds(g * GROUP, GROUP)
        for quadrant in range(4):
            part = memory[wrap(quadrant - x, 4), k, slots]
            rows[:, (quadrant // 2) * CR:(quadrant // 2 + 1) * CR, (quadrant % 2) * QC:(quadrant % 2 + 1) * QC] = part
        here = normed(rows[...].reshape(GROUP * 2 * CR, D_DEC), gain_memory_ref[...])
        for n, result in ((1, keys), (2, values)):
            made = jnp.dot(here, weights_vmem[n], preferred_element_type=F32).astype(BF)
            result[slots, 2 * CR * k:2 * CR * (k + 1)] = made.reshape(GROUP, 2 * CR, D_DEC)

    def attend(g):
        for b in range(GROUP):
            slot = g * GROUP + b
            image = lax.rem(want[0, 0, slot], IMG)
            for p in range(PAIRS_OF_HEADS):
                columns = slice(p * 2 * HEAD, (p + 1) * 2 * HEAD)
                scores = lax.dot_general(stacked[image, p], keys[slot, :, columns], (((1,), (1,)), ((), ())),
                                         preferred_element_type=F32)
                powers = jnp.exp(scores - jnp.max(scores, axis=-1, keepdims=True))
                share = 1.0 / jnp.sum(powers, axis=-1, keepdims=True)
                mixed = jnp.dot((powers * share).astype(BF), values[slot, :, columns], preferred_element_type=F32)
                context[b * TOK:(b + 1) * TOK, columns] = jnp.where(
                    lane < HEAD, mixed[:TOK], mixed[TOK:]).astype(BF)
        projected = jnp.dot(context[...], weights_vmem[3], preferred_element_type=F32)
        for b in range(GROUP):
            slot = g * GROUP + b
            image = lax.rem(want[0, 0, slot], IMG)
            combined = embedded[image].astype(F32) + projected[b * TOK:(b + 1) * TOK]
            decoded_ref[slot] = jnp.where(slot < count_ref[0], combined, 0.0).astype(BF)

    def finish(names):
        def body(g, carry):
            for name in names:
                descriptor(name, g).wait_recv()
            project(CH - 1, g)
            attend(g)
            return carry

        lax.fori_loop(0, SLOTS // GROUP, body, 0)

    run = dict(own=place_own, want=read_wants, sel=select, queries=make_queries, kv=project,
               finish=finish, sent=lambda name: descriptor(name).wait_send(),
               start=lambda name: descriptor(name).start(), wait=lambda name: descriptor(name).wait_recv())
    for what, *which in ORDER:
        run[what](*which)
    for m in MESSAGES:
        if m["link"][0] == "x":
            descriptor(m["name"]).wait_send()


def decode(tokens, embed_weight, gain_query, gain_memory, query_weight, key_weight, value_weight, out_weight, pairs,
           counts):
    vmem = pl.BlockSpec(memory_space=pltpu.VMEM)
    hbm = pl.BlockSpec(memory_space=pl.ANY)
    return pl.pallas_call(
        decode_kernel,
        out_shape=pltpu.VMEM((SLOTS, TOK, D_DEC), BF),
        in_specs=[vmem, vmem, vmem, vmem, hbm, hbm, hbm, hbm, vmem, pl.BlockSpec(memory_space=pltpu.SMEM)],
        out_specs=vmem,
        scratch_shapes=[
            *(pltpu.VMEM((quads, 2, NY, NZ, IMG, CR, QC), BF) for quads in KINDS),
            pltpu.VMEM((CH, 3, SLOTS, CR, QC), BF),
            pltpu.VMEM((SLOTS, CR, QC), BF),
            pltpu.VMEM((4, CH, SLOTS, CR, QC), BF),
            pltpu.VMEM((IMG, TOK, D_DEC), BF),
            pltpu.VMEM((NX, 8, 128), jnp.int32),
            pltpu.SMEM((NX, 8, 128), jnp.int32),
            pltpu.VMEM((4, D_DEC, D_DEC), BF),
            pltpu.VMEM((IMG, PAIRS_OF_HEADS, 2 * TOK, 2 * HEAD), BF),
            pltpu.VMEM((GROUP, 2 * CR, D_DEC), BF),
            pltpu.VMEM((SLOTS, TOK, D_DEC), BF),
            pltpu.VMEM((SLOTS, TOK, D_DEC), BF),
            pltpu.VMEM((GROUP * TOK, D_DEC), BF),
            pltpu.SemaphoreType.DMA((len(MESSAGES),)),
            pltpu.SemaphoreType.DMA((len(MESSAGES),)),
            pltpu.SemaphoreType.DMA((5,)),
        ],
        compiler_params=pltpu.CompilerParams(
            collective_id=0, has_side_effects=True, vmem_limit_bytes=57 * 1024 * 1024
        ),
        name="decode",
    )(tokens, embed_weight, gain_query, gain_memory, query_weight, key_weight, value_weight, out_weight, pairs, counts)


def on_device(
    tokens,
    embed_weight,
    gain_query,
    gain_memory,
    query_weight,
    key_weight,
    value_weight,
    out_weight,
    pair_list,
    counts,
):
    return decode(tokens, embed_weight, gain_query, gain_memory, query_weight, key_weight, value_weight, out_weight,
                  pair_list.T, counts)


def solution(mesh):
    placed = (
        P("img", None, None),
        P(),
        P(),
        P(),
        P(),
        P(),
        P(),
        P(),
        P(("img", "grp"), None),
        P(("img", "grp")),
    )
    return jax.shard_map(
        on_device,
        mesh=mesh,
        in_specs=placed,
        out_specs=P(("img", "grp"), None, None),
        check_vma=False,
    )
```

```python
import functools

import jax
import jax.numpy as jnp
from jax import lax
from jax.experimental import pallas as pl
from jax.experimental.pallas import tpu as pltpu
from jax.sharding import PartitionSpec as P

HEADS = 12
HEAD = 64
D_DEC = 768
D_ENC = 1024
TOK = 96
IMG = 4
SLOTS = 36
EPS = 1e-06

QR = TOK // 2
QC = D_DEC // 2
CH = 3
CR = QR // CH
KINDS = (1, 2, 2)
EARLY = (3, 2, 2)
FINE_Y = (True, True, False)
FINE_Z = (False, False, False)
GROUP = 12

NY, NZ, NX = 4, 8, 4
MESH = pl.DeviceIdType.MESH
BF = jnp.bfloat16
F32 = jnp.float32


def build_messages():
    messages = []
    for d in (1, -1, 2):
        messages.append(dict(name=("wt", 0, d), link=("x", d), size=0.5, after=(), k=0, d=d))

    def add(name, link, size, after, **where):
        messages.append(dict(name=name, link=link, size=size, after=tuple(after), k=name[1], **where))

    hz, hy = NZ // 2, NY // 2

    def part(first, count, far, d):
        if not far:
            return (first, count)
        upper = (count + 1) // 2
        return (first, upper) if d == 1 else (first + upper, count - upper)

    def all_of(legs, fine):
        return legs if fine else {"all": [n for names in legs.values() for n in names]}

    for k in range(CH):
        quads = KINDS[k]
        own = ("own", k)
        early = EARLY[k]
        along_z, along_y = {0: [own]}, {0: [own]}
        for s in range(1, hz + 1):
            for d in (1, -1):
                name, images = ("az", k, d, s), part(0, early, s == hz, d)
                if images[1]:
                    add(name, ("z", d), quads * images[1], [("az", k, d, s - 1)] if s > 1 else [own],
                        y=("one", 0), z=("one", -d * (s - 1)), l=images)
                    along_z.setdefault(hz if s == hz else -d * s, []).append(name)
        for s in range(1, hy + 1):
            for d in (1, -1):
                name, images = ("by", k, d, s), part(early, IMG - early, s == hy, d)
                if images[1]:
                    add(name, ("y", d), quads * images[1], [("by", k, d, s - 1)] if s > 1 else [own],
                        y=("one", -d * (s - 1)), z=("one", 0), l=images)
                    along_y.setdefault(hy if s == hy else -d * s, []).append(name)
        columns, planes = {}, {}
        for s in range(1, hy + 1):
            for d in (1, -1):
                images = part(0, early, s == hy, d)
                for at, arrived in all_of(along_z, FINE_Y[k]).items():
                    name = ("ay", k, d, s, at)
                    if images[1]:
                        add(name, ("y", d), quads * images[1] * (NZ if at == "all" else 1),
                            [("ay", k, d, s - 1, at)] if s > 1 else arrived,
                            y=("one", -d * (s - 1)), z=("all",) if at == "all" else ("one", at), l=images)
                        columns.setdefault(hy if s == hy else -d * s, []).append(name)
        for s in range(1, hz + 1):
            for d in (1, -1):
                images = part(early, IMG - early, s == hz, d)
                for at, arrived in all_of(along_y, FINE_Z[k]).items():
                    name = ("bz", k, d, s, at)
                    if images[1]:
                        add(name, ("z", d), quads * images[1] * (NY if at == "all" else 1),
                            [("bz", k, d, s - 1, at)] if s > 1 else arrived,
                            y=("all",) if at == "all" else ("one", at), z=("one", -d * (s - 1)), l=images)
                        planes.setdefault(hz if s == hz else -d * s, []).append(name)
        columns[0] = [n for at in along_z.values() for n in at]
        planes[0] = [n for at in along_y.values() for n in at]
        for at, arrived in columns.items():
            add(("sa", k, at), ("c", 1), quads * early * NZ, arrived, y=("one", at), z=("all",), l=(0, early))
        for at, arrived in planes.items():
            add(("sb", k, at), ("c", 1), quads * (IMG - early) * NY, arrived, y=("all",), z=("one", at),
                l=(early, IMG - early))
        for g in range(SLOTS // GROUP):
            for d in (1, -1):
                if quads == 1:
                    add(("xf", k, d, g), ("x", d), GROUP // 2, [("sel", k)], g=g, d=d)
            for d in (1, -1):
                add(("xd", k, d, g), ("x", d), GROUP, [("sel", k)], g=g, d=d)
            if quads == 1:
                for d in (1, -1):
                    add(("xx", k, d, g), ("x", d), GROUP // 2, [("xf", k, d, g)], g=g, d=d)
    return messages


LOOK = 3.0
LOOK_X = 2.5
COST = {"sel": 1.0, "queries": 1.5, "kv": 1.2, "attend": 6.0, "want": 0.5}
EVENTS = 8


def build_order(messages):
    rate = {"x": 0.045, "y": 0.045, "z": 0.045, "c": 0.25}
    unit = CR * QC * 2 / 1e6
    rank = {"wt": -1, "by": 0, "az": 0, "bz": 1, "ay": 1}
    waiting = sorted(messages, key=lambda m: (m["k"], rank.get(m["name"][0], 2)))
    done = {("own", k) for k in range(CH)}
    order = [("own", k) for k in range(CH)]
    flying, free, now, since = [], {}, 0.0, 0
    groups = range(SLOTS // GROUP)
    steps = [(("want",), {("wt", 0, d) for d in (1, -1, 2)})]
    for k in range(CH):
        gather = {m["name"] for m in messages if m["k"] == k and m["link"][0] != "x"}
        steps.append((("sel", k), gather | {("want",)}))
    steps.append((("queries",), set()))
    last = CH - 1
    for k in range(last):
        for g in groups:
            here = {m["name"] for m in messages if m["k"] == k and m.get("g") == g and m["name"][0] in ("xd", "xx")}
            steps.append((("kv", k, g), here | {("sel", k)}))
    final = {m["name"] for m in messages if m["k"] == last and m["name"][0] == "xd"}

    def launch():
        rest = []
        for m in waiting:
            at = free.get(m["link"], 0.0)
            look = LOOK if m["link"][0] != "x" else 1e3 if ("sel", last) in done else LOOK_X
            if at - now < look and all(a in done for a in m["after"]):
                end = max(now, at) + m["size"] * unit / rate[m["link"][0]]
                free[m["link"]] = end
                if m["name"] not in final:
                    flying.append((end + 1.5, len(order), m))
                order.append(("start", m["name"]))
            else:
                rest.append(m)
        waiting[:] = rest

    launch()
    while flying or waiting or steps:
        flying.sort(key=lambda f: f[:2])
        ready = [step for step in steps if step[1] <= done]
        ready.sort(key=lambda step: step[0][0] not in ("sel", "want"))
        if ready and (ready[0][0][0] in ("sel", "want") or not flying or flying[0][0] > now + 0.3 or since >= EVENTS):
            name = ready[0][0]
            steps.remove(ready[0])
            order.append(name)
            now += COST[name[0]]
            done.add(name)
            since = 0
            if name == ("sel", last):
                launch()
                order.append(("drain",))
        elif flying:
            t, _, m = flying.pop(0)
            now = max(now, t) + 0.15
            since += 1
            order.append(("wait", m["name"]))
            done.add(m["name"])
        else:
            now += 0.5
        launch()
    order.append(("finish", [("xd", last, d, 0) for d in (1, -1)]))
    return order, now + sum(COST[c] for c in ("kv", "attend")) * len(groups)


MESSAGES = build_messages()
ORDER, MODELLED = build_order(MESSAGES)
NUMBER = {m["name"]: n for n, m in enumerate(MESSAGES)}
PER_GROUP = [6 if quads == 1 else 2 for quads in KINDS]


def wrap(value, size):
    return lax.rem(value + 2 * size, size)


def normed(rows, gain):
    rows = rows.astype(F32)
    centred = rows - jnp.mean(rows, axis=-1, keepdims=True)
    variance = jnp.mean(centred * centred, axis=-1, keepdims=True)
    return (centred * lax.rsqrt(variance + EPS) * gain).astype(BF)


PAIRS_OF_HEADS = HEADS // 2


def decode_kernel(tokens_ref, embed_weight_ref, gain_query_ref, gain_memory_ref, query_weight_hbm, key_weight_hbm,
                  value_weight_hbm, out_weight_hbm, pairs_ref, count_ref, decoded_ref, *scratch):
    gathered = scratch[:CH]
    (out_going, passing, memory, embedded, want_vmem, want, weights_vmem, stacked, rows, keys, values, context,
     send_sem, recv_sem, local_sem) = scratch[CH:]
    img = lax.axis_index("img")
    x = lax.axis_index("grp")
    y = img // (2 * NZ)
    z = lax.rem(img // 2, NZ)
    core = lax.rem(img, 2)

    def device(link):
        axis, d = link
        if axis == "x":
            return (img, wrap(x + d, NX))
        if axis == "y":
            return ((wrap(y + d, NY) * NZ + z) * 2 + core, x)
        if axis == "z":
            return ((y * NZ + wrap(z + d, NZ)) * 2 + core, x)
        return ((y * NZ + z) * 2 + (1 - core), x)

    barrier = pltpu.get_barrier_semaphore()
    partners = [("x", 1), ("x", -1), ("x", 2), ("y", 1), ("y", -1), ("z", 1), ("z", -1), ("c", 1)]
    for link in partners:
        pl.semaphore_signal(barrier, inc=1, device_id=device(link), device_id_type=MESH)

    loads = [pltpu.make_async_copy(hbm, weights_vmem.at[n], local_sem.at[n])
             for n, hbm in enumerate((query_weight_hbm, key_weight_hbm, value_weight_hbm, out_weight_hbm))]
    for load in loads:
        load.start()

    want_vmem[0] = jnp.zeros_like(want_vmem[0])
    want_vmem[0, :2, :SLOTS] = pairs_ref[...]
    embedded[...] = jnp.dot(tokens_ref[...].reshape(IMG * TOK, D_ENC), embed_weight_ref[...],
                            preferred_element_type=F32).astype(BF).reshape(IMG, TOK, D_DEC)

    pl.semaphore_wait(barrier, len(partners))

    def slice_of(m):
        def pick(where, at, size):
            return pl.ds(0, size) if where[0] == "all" else pl.ds(wrap(at + where[1], size), 1)

        first, count = m["l"]
        return gathered[m["k"]].at[pl.ds(0, KINDS[m["k"]]), core, pick(m["y"], y, NY), pick(m["z"], z, NZ),
                                   pl.ds(first, count)]

    def descriptor(name, step=0):
        n = NUMBER[name]
        m = MESSAGES[n]
        kind = name[0]
        half = GROUP // 2
        if kind == "wt":
            src = want_vmem.at[0]
            dst = want_vmem.at[(-m["d"]) % NX]
        elif kind in ("xd", "xf", "xx"):
            k, g, d = m["k"], m["g"] + step, m["d"]
            n = n + step * PER_GROUP[k]
            slots = pl.ds(g * GROUP, GROUP)
            some = pl.ds(g * GROUP + (0 if d == 1 else half), half)
            if kind == "xd":
                src = out_going.at[k, 0 if d == 1 else 1, slots]
                dst = memory.at[(-d) % NX, k, slots]
            elif kind == "xf":
                src = out_going.at[k, 2, some]
                dst = passing.at[some]
            else:
                src = passing.at[some]
                dst = memory.at[2, k, some]
        else:
            src = dst = slice_of(m)
        return pltpu.make_async_remote_copy(
            src_ref=src, dst_ref=dst, send_sem=send_sem.at[n], recv_sem=recv_sem.at[n],
            device_id=device(m["link"]), device_id_type=MESH)

    def place_own(k):
        for q in range(KINDS[k]):
            quadrant = wrap(x + 2 * q, 4)
            row = pl.multiple_of((quadrant // 2) * QR + k * CR, CR)
            column = pl.multiple_of(lax.rem(quadrant, 2) * QC, 128)
            for n in range(IMG):
                gathered[k][q, core, y, z, n] = embedded[n, pl.ds(row, CR), pl.ds(column, QC)]

    def read_wants():
        move = pltpu.make_async_copy(want_vmem, want, local_sem.at[4])
        move.start()
        move.wait()

    def select(k):
        def body(s, carry):
            def read(q, d):
                image = want[d % NX, 1, s]
                owner = image // IMG
                return gathered[k][q, lax.rem(owner, 2), owner // (2 * NZ), lax.rem(owner // 2, NZ),
                                   lax.rem(image, IMG)]

            out_going[k, 0, s] = read(0, 1)
            out_going[k, 1, s] = read(0, -1)
            if KINDS[k] == 1:
                out_going[k, 2, s] = read(0, 2)
            else:
                memory[2, k, s] = read(1, 0)
            memory[0, k, s] = read(0, 0)
            return carry

        lax.fori_loop(0, SLOTS, body, 0)

    lane = lax.broadcasted_iota(jnp.int32, (TOK, 2 * HEAD), 1)

    def make_queries():
        for load in loads:
            load.wait()

        query_rows = jnp.dot(normed(embedded[...].reshape(IMG * TOK, D_DEC), gain_query_ref[...]), weights_vmem[0],
                             preferred_element_type=F32).astype(BF).astype(F32) * HEAD ** (-0.5)
        for n in range(IMG):
            for p in range(PAIRS_OF_HEADS):
                both = query_rows[n * TOK:(n + 1) * TOK, p * 2 * HEAD:(p + 1) * 2 * HEAD]
                stacked[n, p, :TOK] = jnp.where(lane < HEAD, both, 0.0).astype(BF)
                stacked[n, p, TOK:] = jnp.where(lane >= HEAD, both, 0.0).astype(BF)

    def project(k, g):
        slots = pl.ds(g * GROUP, GROUP)
        for quadrant in range(4):
            part = memory[wrap(quadrant - x, 4), k, slots]
            rows[:, (quadrant // 2) * CR:(quadrant // 2 + 1) * CR, (quadrant % 2) * QC:(quadrant % 2 + 1) * QC] = part
        here = normed(rows[...].reshape(GROUP * 2 * CR, D_DEC), gain_memory_ref[...])
        for n, result in ((1, keys), (2, values)):
            made = jnp.dot(here, weights_vmem[n], preferred_element_type=F32).astype(BF)
            result[slots, 2 * CR * k:2 * CR * (k + 1)] = made.reshape(GROUP, 2 * CR, D_DEC)

    def attend(g):
        for b in range(GROUP):
            slot = g * GROUP + b
            image = lax.rem(want[0, 0, slot], IMG)
            for p in range(PAIRS_OF_HEADS):
                columns = slice(p * 2 * HEAD, (p + 1) * 2 * HEAD)
                scores = lax.dot_general(stacked[image, p], keys[slot, :, columns], (((1,), (1,)), ((), ())),
                                         preferred_element_type=F32)
                powers = jnp.exp(scores - jnp.max(scores, axis=-1, keepdims=True))
                share = 1.0 / jnp.sum(powers, axis=-1, keepdims=True)
                mixed = jnp.dot((powers * share).astype(BF), values[slot, :, columns], preferred_element_type=F32)
                context[b * TOK:(b + 1) * TOK, columns] = jnp.where(
                    lane < HEAD, mixed[:TOK], mixed[TOK:]).astype(BF)
        projected = jnp.dot(context[...], weights_vmem[3], preferred_element_type=F32)
        for b in range(GROUP):
            slot = g * GROUP + b
            image = lax.rem(want[0, 0, slot], IMG)
            combined = embedded[image].astype(F32) + projected[b * TOK:(b + 1) * TOK]
            decoded_ref[slot] = jnp.where(slot < count_ref[0], combined, 0.0).astype(BF)

    def drain():
        for m in MESSAGES:
            if m["link"][0] != "x":
                descriptor(m["name"]).wait_send()

    def finish(names):
        def body(g, carry):
            for name in names:
                descriptor(name, g).wait_recv()
            project(CH - 1, g)
            attend(g)
            return carry

        lax.fori_loop(0, SLOTS // GROUP, body, 0)

    run = dict(own=place_own, want=read_wants, sel=select, queries=make_queries, kv=project,
               finish=finish, drain=drain,
               start=lambda name: descriptor(name).start(), wait=lambda name: descriptor(name).wait_recv())
    for what, *which in ORDER:
        run[what](*which)
    for m in MESSAGES:
        if m["link"][0] == "x":
            descriptor(m["name"]).wait_send()


def decode(tokens, embed_weight, gain_query, gain_memory, query_weight, key_weight, value_weight, out_weight, pairs,
           counts):
    vmem = pl.BlockSpec(memory_space=pltpu.VMEM)
    hbm = pl.BlockSpec(memory_space=pl.ANY)
    return pl.pallas_call(
        decode_kernel,
        out_shape=pltpu.VMEM((SLOTS, TOK, D_DEC), BF),
        in_specs=[vmem, vmem, vmem, vmem, hbm, hbm, hbm, hbm, vmem, pl.BlockSpec(memory_space=pltpu.SMEM)],
        out_specs=vmem,
        scratch_shapes=[
            *(pltpu.VMEM((quads, 2, NY, NZ, IMG, CR, QC), BF) for quads in KINDS),
            pltpu.VMEM((CH, 3, SLOTS, CR, QC), BF),
            pltpu.VMEM((SLOTS, CR, QC), BF),
            pltpu.VMEM((4, CH, SLOTS, CR, QC), BF),
            pltpu.VMEM((IMG, TOK, D_DEC), BF),
            pltpu.VMEM((NX, 8, 128), jnp.int32),
            pltpu.SMEM((NX, 8, 128), jnp.int32),
            pltpu.VMEM((4, D_DEC, D_DEC), BF),
            pltpu.VMEM((IMG, PAIRS_OF_HEADS, 2 * TOK, 2 * HEAD), BF),
            pltpu.VMEM((GROUP, 2 * CR, D_DEC), BF),
            pltpu.VMEM((SLOTS, TOK, D_DEC), BF),
            pltpu.VMEM((SLOTS, TOK, D_DEC), BF),
            pltpu.VMEM((GROUP * TOK, D_DEC), BF),
            pltpu.SemaphoreType.DMA((len(MESSAGES),)),
            pltpu.SemaphoreType.DMA((len(MESSAGES),)),
            pltpu.SemaphoreType.DMA((5,)),
        ],
        compiler_params=pltpu.CompilerParams(
            collective_id=0, has_side_effects=True, vmem_limit_bytes=57 * 1024 * 1024
        ),
        name="decode",
    )(tokens, embed_weight, gain_query, gain_memory, query_weight, key_weight, value_weight, out_weight, pairs, counts)


def on_device(
    tokens,
    embed_weight,
    gain_query,
    gain_memory,
    query_weight,
    key_weight,
    value_weight,
    out_weight,
    pair_list,
    counts,
):
    return decode(tokens, embed_weight, gain_query, gain_memory, query_weight, key_weight, value_weight, out_weight,
                  pair_list.T, counts)


def solution(mesh):
    placed = (
        P("img", None, None),
        P(),
        P(),
        P(),
        P(),
        P(),
        P(),
        P(),
        P(("img", "grp"), None),
        P(("img", "grp")),
    )
    return jax.shard_map(
        on_device,
        mesh=mesh,
        in_specs=placed,
        out_specs=P(("img", "grp"), None, None),
        check_vma=False,
    )
```
